32 devices in a mesh: section: 2 (over x), dp: 8 (over z, core), seq: 2 (over y).
Axes of the slice: x: 2, y: 2, z: 4, core: 2. Of those that a mesh axis runs over, the one named last changes fastest.
Arguments:
- section_input: bfloat16 [2, 2048, 5120], P('section', 'seq', 'dp'), as said below
- norm_gain: bfloat16 [2, 5120], P('section', 'dp'), may hold values from 0.5 to 2
- qkv_weight: bfloat16 [2, 5120, 3072], P('section', 'seq', 'dp'), as said below
- out_weight: bfloat16 [2, 1024, 5120], P('section', None, 'dp'), may hold values from -1 to 1
- random_blocks: int32 [2, 32, 3], P('section', 'seq'), may hold values from 0 to 31
- global_blocks: int32 [2, 2], P('section'), may hold values from 0 to 31, as said below
Outputs:
- handed_on: bfloat16 [2, 2048, 5120], P('section', 'seq', 'dp')
The draws below stay inside these ranges and needn't reach their ends.
Inputs may be any that keep to these rules, and one draw needn't show every extreme that they name: `section_input`: real values, each token row and each feature column with its own scale. `qkv_weight`: real values of projections. `global_blocks`: 2 different block numbers for each section; the last section's document has the first and the last block as its global blocks.
All inputs are finite; a program needn't handle non-finite values.
Results may differ from the reference program's by a relative error of at most 0.0058.
Values may be sent and summed in bfloat16 or wider, within the bound.
A program may use at most 64 MiB of HBM per device.

```python
import math
import jax
import jax.numpy as jnp
from jax import lax

D = 5120
HD = 128
BLOCK = 64
RANDOMS = 3
GLOBALS = 2
TOKENS = 2048
NB = 32
HEADS = 8
SECTIONS = 2


def draw_section_input(key, part):
    base_key, row_key, col_key = jax.random.split(key, 3)
    base = jnp.clip(jax.random.normal(base_key, (SECTIONS, TOKENS, D), jnp.float32), -6.0, 6.0)
    row_scale = jnp.exp(jax.random.uniform(row_key, (SECTIONS, TOKENS, 1), jnp.float32, math.log(0.3), math.log(3.0)))
    col_scale = jnp.exp(jax.random.uniform(col_key, (SECTIONS, 1, D), jnp.float32, math.log(0.4), math.log(4.0)))
    position = jnp.arange(D, dtype=jnp.float32) / (D - 1)
    ramp = jnp.exp(0.5 * math.log(3.0) * position)
    values = base * row_scale * col_scale * ramp[None, None, :]
    return values.astype(jnp.bfloat16)


def draw_qkv_weight(key, part):
    raw_key = jax.random.fold_in(key, 0)
    raw = jnp.clip(jax.random.normal(raw_key, (SECTIONS, D, HEADS, 3, HD), jnp.float32), -6.0, 6.0)
    factor = jnp.array([1.2, 1.2, 1.0], jnp.float32)[None, None, None, :, None]
    full = raw * factor / math.sqrt(D)
    return full.reshape(SECTIONS, D, HEADS * 3 * HD).astype(jnp.bfloat16)


def draw_global_blocks(key, part):
    section_keys = jax.random.split(jax.random.fold_in(key, 17), SECTIONS)

    def pick(one_key):
        return jax.random.permutation(one_key, NB)[:GLOBALS].astype(jnp.int32)
    picked = jax.vmap(pick)(section_keys)
    ends = jnp.zeros((GLOBALS,), jnp.int32).at[GLOBALS - 1].set(NB - 1)
    is_last = (jnp.arange(SECTIONS, dtype=jnp.int32) == SECTIONS - 1)[:, None]
    return jnp.where(is_last, ends[None, :], picked).astype(jnp.int32)


def place_ends(entries, stream_key, low, top_value):
    extent = entries.shape
    spot = [jax.random.randint(jax.random.fold_in(stream_key, axis), (), 0, extent[axis]) for axis in range(len(extent))]
    entries = entries.at[tuple(spot)].set(low)
    longest = extent.index(max(extent))
    spot[longest] = (spot[longest] + 1) % extent[longest]
    return entries.at[tuple(spot)].set(top_value)


def level_of(key, dims, shards, low, top_value):
    level, own = 1.0, jax.random.fold_in(key, 6)
    for axis_at, parts in shards:
        heights = jnp.exp(jax.random.uniform(jax.random.fold_in(own, axis_at), (parts,), jnp.float32, low / len(shards), top_value / len(shards)))
        level = level * jnp.repeat(heights, dims[axis_at] // parts).reshape([-1 if axis == axis_at else 1 for axis in range(len(dims))])
    return level


def bell_draw(key, dims, deviation, bound, cuts=(), held_as=jnp.bfloat16):
    drawn = deviation * jax.random.normal(key, dims, jnp.float32)
    if cuts:
        drawn = drawn * level_of(key, dims, cuts, -0.22, 0.18)
    return jnp.clip(drawn, -bound, bound).astype(held_as)


def setup_inputs(seed: int = 0) -> dict:
    key_list = jax.random.split(jax.random.key(seed), 7)
    section_input = draw_section_input(jax.random.fold_in(key_list[6], 71), 0)
    norm_gain = jnp.clip(jnp.exp(math.log(2.0) - 1.3862944 * jax.random.uniform(key_list[1], (SECTIONS, D), jnp.float32) ** level_of(key_list[1], (SECTIONS, D), ((0, 2), (1, 8)), -0.2, 0.2)), 0.5, 2.0).astype(jnp.bfloat16)
    qkv_weight = draw_qkv_weight(jax.random.fold_in(key_list[6], 71), 0)
    out_weight = bell_draw(key_list[3], (SECTIONS, HEADS * HD, D), (HEADS * HD // 32) ** -0.5, 1.0, ((0, 2), (2, 8)))
    random_blocks = place_ends(jax.random.randint(key_list[4], (SECTIONS, NB, RANDOMS), 0, NB), jax.random.fold_in(key_list[4], 1), 0, NB - 1).astype(jnp.int32)
    global_blocks = draw_global_blocks(jax.random.fold_in(key_list[6], 71), 0)
    return {"section_input": section_input, "norm_gain": norm_gain, "qkv_weight": qkv_weight, "out_weight": out_weight, "random_blocks": random_blocks, "global_blocks": global_blocks}


def block_mask(query_ids, random_rows, global_ids, key_count):
    query_col = query_ids[:, None]
    key_ids = jnp.arange(key_count, dtype=jnp.int32)[None, :]
    adjacent = jnp.abs(query_col - key_ids) <= 1
    key_global = jnp.any(key_ids[:, :, None] == global_ids[None, None, :], axis=2)
    query_global = jnp.any(query_col[:, :, None] == global_ids[None, None, :], axis=2)
    chosen = jnp.any(random_rows[:, None, :] == key_ids[:, :, None], axis=2)
    return adjacent | key_global | query_global | chosen

def sparse_attention(query, keys, values, allowed, block_size):
    scores = lax.dot_general(query, keys, (((1,), (1,)), ((), ())), preferred_element_type=jnp.float32)
    scores = scores * (1.0 / math.sqrt(query.shape[1]))
    query_blocks, key_blocks = allowed.shape
    scores = scores.reshape(query_blocks, block_size, key_blocks, block_size)
    live = allowed[:, None, :, None]
    scores = jnp.where(live, scores, -1e+30)
    highest = lax.optimization_barrier(jnp.max(scores, axis=(2, 3), keepdims=True))
    weights = jnp.where(live, jnp.exp(scores - highest), 0.0)
    totals = lax.optimization_barrier(jnp.sum(weights, axis=(2, 3), keepdims=True))
    probs = (weights / totals).reshape(query_blocks * block_size, key_blocks * block_size).astype(jnp.bfloat16)
    return jnp.dot(probs, values, preferred_element_type=jnp.float32).astype(jnp.bfloat16)

def section_layer(activations, gain, projection, out_proj, random_rows, global_ids):
    length = activations.shape[0]
    as_float = activations.astype(jnp.float32)
    mean_sq = lax.optimization_barrier(jnp.mean(as_float * as_float, axis=1, keepdims=True))
    normed = (as_float * lax.rsqrt(mean_sq + 1e-05) * gain.astype(jnp.float32)).astype(jnp.bfloat16)
    joined = jnp.dot(normed, projection, preferred_element_type=jnp.float32)
    count = length // BLOCK
    allowed = block_mask(jnp.arange(count, dtype=jnp.int32), random_rows, global_ids, count)
    pieces = joined.reshape(length, HEADS, 3, HD).astype(jnp.bfloat16)
    pieces = jnp.transpose(pieces, (1, 2, 0, 3))

    def one_head(item):
        return sparse_attention(item[0], item[1], item[2], allowed, BLOCK)
    head_results = lax.map(one_head, pieces)
    attended = jnp.transpose(head_results, (1, 0, 2)).reshape(length, HEADS * HD)
    added = jnp.dot(attended, out_proj, preferred_element_type=jnp.float32)
    return (as_float + added).astype(jnp.bfloat16)

def reference(section_input, norm_gain, qkv_weight, out_weight, random_blocks, global_blocks):
    results = []
    for section_index in range(SECTIONS):
        results.append(section_layer(section_input[section_index], norm_gain[section_index], qkv_weight[section_index], out_weight[section_index], random_blocks[section_index], global_blocks[section_index]))
    return jnp.roll(jnp.stack(results), 1, axis=0)
```

```python
import functools
import math

import jax
import jax.numpy as jnp
from jax import lax
from jax.experimental import pallas as pl
from jax.experimental.pallas import tpu as pltpu
from jax.sharding import PartitionSpec as P

BLOCK = 64


def shifted(block, axis, distance):
    devices = range(lax.axis_size(axis))
    route = [((i - distance) % len(devices), i) for i in devices]
    return lax.ppermute(block, axis, route)


def block_mask(query_ids, random_rows, global_ids, key_count):
    query_col = query_ids[:, None]
    key_ids = jnp.arange(key_count, dtype=jnp.int32)[None, :]
    adjacent = jnp.abs(query_col - key_ids) <= 1
    key_global = jnp.any(key_ids[:, :, None] == global_ids[None, None, :], axis=2)
    query_global = jnp.any(query_col[:, :, None] == global_ids[None, None, :], axis=2)
    chosen = jnp.any(random_rows[:, None, :] == key_ids[:, :, None], axis=2)
    return adjacent | key_global | query_global | chosen


def sparse_attention(query, keys, values, allowed, block_size):
    scores = lax.dot_general(
        query, keys, (((1,), (1,)), ((), ())), preferred_element_type=jnp.float32
    )
    scores = scores * (1.0 / math.sqrt(query.shape[1]))
    query_blocks, key_blocks = allowed.shape
    scores = scores.reshape(query_blocks, block_size, key_blocks, block_size)
    live = allowed[:, None, :, None]
    scores = jnp.where(live, scores, -1e30)
    highest = jnp.max(scores, axis=(2, 3), keepdims=True)
    weights = jnp.where(live, jnp.exp(scores - highest), 0.0)
    totals = jnp.sum(weights, axis=(2, 3), keepdims=True)
    probs = (
        (weights / totals)
        .reshape(query_blocks * block_size, key_blocks * block_size)
        .astype(jnp.bfloat16)
    )
    return jnp.dot(probs, values, preferred_element_type=jnp.float32).astype(jnp.bfloat16)


def shards(section_input, norm_gain, qkv_weight, out_weight, random_blocks, global_blocks):
    token_rows = section_input[0]
    token_count = token_rows.shape[0]
    width = norm_gain.shape[1] * lax.axis_size("dp")
    as_float = token_rows.astype(jnp.float32)
    local_squares = jnp.sum(as_float * as_float, axis=1)
    total_squares = lax.psum(local_squares, "dp")
    factor = lax.rsqrt(total_squares / width + 1e-05)[:, None]
    normed_part = (as_float * factor * norm_gain[0].astype(jnp.float32)).astype(jnp.bfloat16)
    normed = lax.all_gather(normed_part, "dp", axis=1, tiled=True)
    weight_half = qkv_weight[0]
    joined = jnp.dot(
        normed,
        lax.all_gather(weight_half, "seq", axis=0, tiled=True),
        preferred_element_type=jnp.float32,
    )
    head_size = joined.shape[1] // 3
    query = joined[:, :head_size].astype(jnp.bfloat16)
    keys_values = joined[:, head_size:].astype(jnp.bfloat16)
    document_kv = lax.all_gather(keys_values, "seq", axis=0, tiled=True)
    keys = document_kv[:, :head_size]
    values = document_kv[:, head_size:]
    own_blocks = token_count // BLOCK
    query_ids = lax.axis_index("seq") * own_blocks + jnp.arange(own_blocks, dtype=jnp.int32)
    allowed = block_mask(
        query_ids, random_blocks[0], global_blocks[0], document_kv.shape[0] // BLOCK
    )
    attended = sparse_attention(query, keys, values, allowed, BLOCK)
    out_columns = out_weight[0]
    added = jnp.dot(
        lax.all_gather(attended, "dp", axis=1, tiled=True),
        out_columns,
        preferred_element_type=jnp.float32,
    )
    result = (token_rows.astype(jnp.float32) + added).astype(jnp.bfloat16)
    return shifted(result[None], "section", 1)


CHUNKS = 4


def relay_kernel(
    nz,
    x_ref,
    gain_ref,
    w_ref,
    ow_ref,
    rand_ref,
    glob_ref,
    out_ref,
    x_all,
    w_all,
    g_all,
    acc,
    squares,
    q_s,
    kv,
    bias,
    m_s,
    l_s,
    o_s,
    att_own,
    att_all,
    x_next,
    ow_next,
    xs,
    xr,
    ws,
    wr,
    gs,
    gr,
    ks,
    kr,
    ts,
    tr,
    as_,
    ar,
    ns,
    nr,
    local,
):
    sec, p, y = lax.axis_index("section"), lax.axis_index("dp"), lax.axis_index("seq")
    dp = 2 * nz
    z, core = p // 2, p % 2
    sib = p + 1 - 2 * core
    tokens, feats = x_ref.shape
    width = feats * dp
    rows = tokens // CHUNKS
    head = q_s.shape[1]
    half = dp // 2
    scale = math.log2(math.e) / math.sqrt(head)

    barrier = pltpu.get_barrier_semaphore()
    for step in range(1, dp):
        pl.semaphore_signal(
            barrier, inc=1, device_id={"dp": lax.rem(p + step, dp)},
            device_id_type=pl.DeviceIdType.MESH,
        )
    for name, at in (("seq", 1 - y), ("section", 1 - sec)):
        pl.semaphore_signal(
            barrier, inc=1, device_id={name: at}, device_id_type=pl.DeviceIdType.MESH
        )

    def remote(src, dst, send, recv, where):
        return pltpu.make_async_remote_copy(
            src_ref=src, dst_ref=dst, send_sem=send, recv_sem=recv,
            device_id=where, device_id_type=pl.DeviceIdType.MESH,
        )

    def part(k):
        return pl.ds(k * rows, rows)

    def chunk(k):
        return pl.ds(pl.multiple_of(k * rows, rows), rows)

    own_x = pltpu.make_async_copy(x_ref, x_all.at[p], local.at[0])
    own_w = pltpu.make_async_copy(
        w_ref, w_all.at[pl.ds(pl.multiple_of(y * half * feats, feats), half * feats), :], local.at[1]
    )
    own_x.start()
    own_w.start()
    g_all[p] = jnp.broadcast_to(gain_ref[...].astype(jnp.float32), (8, feats))

    pl.semaphore_wait(barrier, dp + 1)

    def hop(buf, send, recv, way, b, k, src=None):
        at = buf.at[b, part(k), :]
        to = (p - 2, p + 2, sib)[way]
        return remote(at if src is None else src, at, send.at[way, b, k], recv.at[b, k], {"dp": to})

    def spread(buf, send, recv, b, k, ways, act, src=None):
        if 0 in ways:
            @pl.when(z > 0)
            def _():
                act(hop(buf, send, recv, 0, b, k, src))
        if 1 in ways:
            @pl.when(z < nz - 1)
            def _():
                act(hop(buf, send, recv, 1, b, k, src))
        act(hop(buf, send, recv, 2, b, k, src))

    start = lambda copy: copy.start()
    sent = lambda copy: copy.wait_send()

    def chain(buf, send, recv, d, k):
        @pl.when(z + d < nz)
        def _():
            b = p + 2 * d
            hop(buf, send, recv, 2, b, k).wait_recv()
            spread(buf, send, recv, b, k, (0,), start)

        @pl.when(z - d >= 0)
        def _():
            b = p - 2 * d
            hop(buf, send, recv, 2, b, k).wait_recv()
            spread(buf, send, recv, b, k, (1,), start)

    def drain(buf, send, recv, k, src=None):
        spread(buf, send, recv, p, k, (0, 1), sent, src)
        for d in range(1, nz):
            @pl.when(z + d < nz)
            def _():
                spread(buf, send, recv, p + 2 * d, k, (0,), sent)

            @pl.when(z - d >= 0)
            def _():
                spread(buf, send, recv, p - 2 * d, k, (1,), sent)

    for k in range(CHUNKS):
        spread(x_all, xs, xr, p, k, (0, 1), start, x_ref.at[part(k), :])

    def gain_copy(to, src):
        return remote(g_all.at[src], g_all.at[src], gs.at[to], gr.at[src], {"dp": to})

    for step in range(1, dp):
        gain_copy(lax.rem(p + step, dp), p).start()

    flip = jnp.where(y == 0, jnp.where(z >= 1, 1, 0), jnp.where(z >= nz - 1, 1, 0)) * (half // 2)

    def w_copy(j, whose):
        block = lax.rem(j + flip, half) if whose is None else whose
        mine = pl.ds(pl.multiple_of(block * feats, feats), feats)
        there = pl.ds(pl.multiple_of((y * half + block) * feats, feats), feats)
        return remote(w_ref.at[mine, :], w_all.at[there, :], ws.at[block], wr.at[block], {"seq": 1 - y})

    for j in range(half):
        w_copy(j, None).start()

    next_x = remote(x_ref, x_next, ns.at[0], nr.at[0], {"section": 1 - sec})
    next_w = remote(ow_ref, ow_next, ns.at[1], nr.at[1], {"section": 1 - sec})
    next_x.start()
    next_w.start()

    acc[...] = jnp.zeros_like(acc)
    squares[...] = jnp.zeros_like(squares)

    blocks = tokens // BLOCK
    for h in range(2):
        key_at = y if h == 0 else 1 - y
        lane = lax.broadcasted_iota(jnp.int32, (blocks, tokens), 1)
        key_id = lane // BLOCK + key_at * blocks
        query_id = lax.broadcasted_iota(jnp.int32, (blocks, tokens), 0) + y * blocks
        allowed = jnp.abs(query_id - key_id) <= 1
        for g in range(glob_ref.shape[1]):
            number = glob_ref[:, g : g + 1]
            allowed = allowed | (key_id == number) | (query_id == number)
        for r in range(rand_ref.shape[1]):
            allowed = allowed | (key_id == rand_ref[:, r : r + 1])
        bias[h] = jnp.where(allowed, 0.0, -jnp.inf)

    def project(b, k):
        xb = x_all[b, chunk(k), :].astype(jnp.float32)
        sq = xb * xb
        folded = sq[:, :128]
        for c in range(1, feats // 128):
            folded = folded + sq[:, c * 128 : (c + 1) * 128]
        squares[chunk(k), :] += folded
        xg = (xb * g_all[b, 0:1, :]).astype(jnp.bfloat16)
        wb = w_all[pl.ds(pl.multiple_of(b * feats, feats), feats), :]
        acc[chunk(k), :] += jnp.dot(xg, wb, preferred_element_type=jnp.float32)

    def ready(b):
        @pl.when(b != p)
        def _():
            gain_copy(sib, b).wait_recv()

        @pl.when(b // half != y)
        def _():
            w_copy(0, b % half).wait_recv()

    def each(d, fn):
        if d == 0:
            fn(p, False)
            fn(sib, True)
            return

        @pl.when(z + d < nz)
        def _():
            fn(p + 2 * d, False)
            fn(sib + 2 * d, True)

        @pl.when(z - d >= 0)
        def _():
            fn(p - 2 * d, False)
            fn(sib - 2 * d, True)

    def from_sib(b, k):
        hop(x_all, xs, xr, 2, b, k).wait_recv()

    def whole_step(d):
        def one(b, other):
            ready(b)
            if other:
                for k in range(CHUNKS):
                    from_sib(b, k)

            def body(k, _):
                project(b, k)
                return 0

            lax.fori_loop(0, CHUNKS, body, 0)

        each(d, one)

    def kv_copy(k):
        return remote(kv.at[0, part(k), :], kv.at[1, part(k), :], ks.at[k], kr.at[k], {"seq": 1 - y})

    def last_step(k):
        def one(b, other):
            if k == 0:
                ready(b)
            if other:
                from_sib(b, k)
            project(b, k)

        if nz > 1:
            each(nz - 1, one)
        total = jnp.sum(squares[part(k), :], axis=1, keepdims=True)
        joined = acc[part(k), :] * lax.rsqrt(total / width + 1e-05)
        q_s[part(k), :] = joined[:, :head].astype(jnp.bfloat16)
        kv[0, part(k), :] = joined[:, head:].astype(jnp.bfloat16)
        kv_copy(k).start()

    own_x.wait()
    own_w.wait()
    for d in range(1, nz):
        for k in range(CHUNKS):
            chain(x_all, xs, xr, d, k)
            if d == nz - 2 and k == 1:
                for e in range(0, nz - 3):
                    whole_step(e)
            if d == nz - 2 and k == 2:
                whole_step(nz - 3)
            if d == nz - 1 and k == 0:
                whole_step(nz - 2)
            if d == nz - 1 and k > 0:
                last_step(k - 1)
    last_step(CHUNKS - 1)

    per = blocks // CHUNKS

    def scores_of(k, h):
        s = lax.dot_general(
            q_s[part(k), :], kv[h, :, :head], (((1,), (1,)), ((), ())),
            preferred_element_type=jnp.float32,
        )
        s = (s * scale).reshape(per, BLOCK, tokens)
        s = s + bias[h, k * per : (k + 1) * per, :][:, None, :]
        return s.reshape(rows, tokens)

    def own_keys(k):
        s = scores_of(k, 0)
        m = jnp.max(s, axis=1, keepdims=True)
        e = jnp.exp2(s - m)
        m_s[part(k), :] = m
        l_s[part(k), :] = jnp.sum(e, axis=1, keepdims=True)
        o_s[part(k), :] = jnp.dot(
            e.astype(jnp.bfloat16), kv[0, :, head:], preferred_element_type=jnp.float32
        )

    def att_copy(k):
        return remote(
            att_own.at[part(k), :], att_all.at[p, part(k), :], ts.at[k], ar.at[p, k], {"section": 1 - sec}
        )

    def other_keys(k):
        s = scores_of(k, 1)
        before = m_s[part(k), :]
        m = jnp.maximum(before, jnp.max(s, axis=1, keepdims=True))
        e = jnp.exp2(s - m)
        shrink = jnp.exp2(before - m)
        total = l_s[part(k), :] * shrink + jnp.sum(e, axis=1, keepdims=True)
        o = o_s[part(k), :] * shrink + jnp.dot(
            e.astype(jnp.bfloat16), kv[1, :, head:], preferred_element_type=jnp.float32
        )
        att_own[part(k), :] = (o / total).astype(jnp.bfloat16)
        att_copy(k).start()

    for k in range(CHUNKS):
        own_keys(k)
    for k in range(CHUNKS):
        kv_copy(k).wait_recv()
    next_x.wait_recv()
    next_w.wait_recv()

    def att_step(d, k):
        if d == 0:
            att_copy(k).wait_recv()
            spread(att_all, as_, ar, p, k, (0, 1), start)
        else:
            chain(att_all, as_, ar, d, k)

    def finish(k):
        hop(att_all, as_, ar, 2, sib, k).wait_recv()
        for d in range(1, nz):
            @pl.when(z + d < nz)
            def _():
                hop(att_all, as_, ar, 2, sib + 2 * d, k).wait_recv()

            @pl.when(z - d >= 0)
            def _():
                hop(att_all, as_, ar, 2, sib - 2 * d, k).wait_recv()
        heads = jnp.concatenate([att_all[b, part(k), :] for b in range(dp)], axis=1)
        added = jnp.dot(heads, ow_next[...], preferred_element_type=jnp.float32)
        out_ref[part(k), :] = (x_next[part(k), :].astype(jnp.float32) + added).astype(jnp.bfloat16)

    for i in range(CHUNKS + nz + 1):
        if i < CHUNKS:
            other_keys(i)
        for d in range(nz):
            if 0 <= i - 1 - d < CHUNKS:
                att_step(d, i - 1 - d)
        if 0 <= i - nz - 1 < CHUNKS:
            finish(i - nz - 1)

    for k in range(CHUNKS):
        drain(x_all, xs, xr, k)
        drain(att_all, as_, ar, k)
        kv_copy(k).wait_send()
        att_copy(k).wait_send()
    for step in range(1, dp):
        gain_copy(lax.rem(p + step, dp), p).wait_send()
    for j in range(half):
        w_copy(j, None).wait_send()
    next_x.wait_send()
    next_w.wait_send()


def relay(dp, x, gain, w, ow, rand, glob):
    nz = dp // 2
    tokens, feats = x.shape
    columns = w.shape[1]
    head = columns // 3
    vmem = pl.BlockSpec(memory_space=pltpu.VMEM)
    anywhere = pl.BlockSpec(memory_space=pl.ANY)
    bf16, f32, dma = jnp.bfloat16, jnp.float32, pltpu.SemaphoreType.DMA
    return pl.pallas_call(
        functools.partial(relay_kernel, nz),
        out_shape=jax.ShapeDtypeStruct((tokens, feats), bf16),
        in_specs=[anywhere, vmem, anywhere, anywhere, vmem, vmem],
        out_specs=vmem,
        scratch_shapes=[
            pltpu.VMEM((dp, tokens, feats), bf16),
            pltpu.VMEM((dp * feats, columns), bf16),
            pltpu.VMEM((dp, 8, feats), f32),
            pltpu.VMEM((tokens, columns), f32),
            pltpu.VMEM((tokens, 128), f32),
            pltpu.VMEM((tokens, head), bf16),
            pltpu.VMEM((2, tokens, 2 * head), bf16),
            pltpu.VMEM((2, tokens // BLOCK, tokens), f32),
            pltpu.VMEM((tokens, 1), f32),
            pltpu.VMEM((tokens, 1), f32),
            pltpu.VMEM((tokens, head), f32),
            pltpu.VMEM((tokens, head), bf16),
            pltpu.VMEM((dp, tokens, head), bf16),
            pltpu.VMEM((tokens, feats), bf16),
            pltpu.VMEM(ow.shape, bf16),
            dma((3, dp, CHUNKS)),
            dma((dp, CHUNKS)),
            dma((dp // 2,)),
            dma((dp // 2,)),
            dma((dp,)),
            dma((dp,)),
            dma((CHUNKS,)),
            dma((CHUNKS,)),
            dma((CHUNKS,)),
            dma((CHUNKS,)),
            dma((3, dp, CHUNKS)),
            dma((dp, CHUNKS)),
            dma((2,)),
            dma((2,)),
            dma((2,)),
        ],
        compiler_params=pltpu.CompilerParams(
            collective_id=0, has_side_effects=True, vmem_limit_bytes=56 * 1024 * 1024
        ),
        name="relay_layer",
    )(x, gain, w, ow, rand, glob)


def tiles(mesh, tokens, feats, columns):
    return (
        mesh.shape["section"] == 2
        and mesh.shape["seq"] == 2
        and mesh.shape["dp"] == 8
        and feats % 128 == 0
        and columns % 384 == 0
        and tokens % (CHUNKS * BLOCK) == 0
    )


def solution(mesh):
    placed = (
        P("section", "seq", "dp"),
        P("section", "dp"),
        P("section", "seq", "dp"),
        P("section", None, "dp"),
        P("section", "seq", None),
        P("section", None),
    )

    def layer(section_input, norm_gain, qkv_weight, out_weight, random_blocks, global_blocks):
        args = (section_input, norm_gain, qkv_weight, out_weight, random_blocks, global_blocks)
        _, tokens, feats = section_input.shape
        if not tiles(mesh, tokens, feats, qkv_weight.shape[2]):
            return shards(*args)
        out = relay(
            mesh.shape["dp"], section_input[0], norm_gain, qkv_weight[0], out_weight[0],
            random_blocks[0], global_blocks,
        )
        return out[None]

    return jax.shard_map(
        layer, mesh=mesh, in_specs=placed, out_specs=P("section", "seq", "dp"), check_vma=False
    )
```

```python
import functools
import math

import jax
import jax.numpy as jnp
from jax import lax
from jax.experimental import pallas as pl
from jax.experimental.pallas import tpu as pltpu
from jax.sharding import PartitionSpec as P

BLOCK = 64


def shifted(block, axis, distance):
    devices = range(lax.axis_size(axis))
    route = [((i - distance) % len(devices), i) for i in devices]
    return lax.ppermute(block, axis, route)


def block_mask(query_ids, random_rows, global_ids, key_count):
    query_col = query_ids[:, None]
    key_ids = jnp.arange(key_count, dtype=jnp.int32)[None, :]
    adjacent = jnp.abs(query_col - key_ids) <= 1
    key_global = jnp.any(key_ids[:, :, None] == global_ids[None, None, :], axis=2)
    query_global = jnp.any(query_col[:, :, None] == global_ids[None, None, :], axis=2)
    chosen = jnp.any(random_rows[:, None, :] == key_ids[:, :, None], axis=2)
    return adjacent | key_global | query_global | chosen


def sparse_attention(query, keys, values, allowed, block_size):
    scores = lax.dot_general(
        query, keys, (((1,), (1,)), ((), ())), preferred_element_type=jnp.float32
    )
    scores = scores * (1.0 / math.sqrt(query.shape[1]))
    query_blocks, key_blocks = allowed.shape
    scores = scores.reshape(query_blocks, block_size, key_blocks, block_size)
    live = allowed[:, None, :, None]
    scores = jnp.where(live, scores, -1e30)
    highest = jnp.max(scores, axis=(2, 3), keepdims=True)
    weights = jnp.where(live, jnp.exp(scores - highest), 0.0)
    totals = jnp.sum(weights, axis=(2, 3), keepdims=True)
    probs = (
        (weights / totals)
        .reshape(query_blocks * block_size, key_blocks * block_size)
        .astype(jnp.bfloat16)
    )
    return jnp.dot(probs, values, preferred_element_type=jnp.float32).astype(jnp.bfloat16)


def shards(section_input, norm_gain, qkv_weight, out_weight, random_blocks, global_blocks):
    token_rows = section_input[0]
    token_count = token_rows.shape[0]
    width = norm_gain.shape[1] * lax.axis_size("dp")
    as_float = token_rows.astype(jnp.float32)
    local_squares = jnp.sum(as_float * as_float, axis=1)
    total_squares = lax.psum(local_squares, "dp")
    factor = lax.rsqrt(total_squares / width + 1e-05)[:, None]
    normed_part = (as_float * factor * norm_gain[0].astype(jnp.float32)).astype(jnp.bfloat16)
    normed = lax.all_gather(normed_part, "dp", axis=1, tiled=True)
    weight_half = qkv_weight[0]
    joined = jnp.dot(
        normed,
        lax.all_gather(weight_half, "seq", axis=0, tiled=True),
        preferred_element_type=jnp.float32,
    )
    head_size = joined.shape[1] // 3
    query = joined[:, :head_size].astype(jnp.bfloat16)
    keys_values = joined[:, head_size:].astype(jnp.bfloat16)
    document_kv = lax.all_gather(keys_values, "seq", axis=0, tiled=True)
    keys = document_kv[:, :head_size]
    values = document_kv[:, head_size:]
    own_blocks = token_count // BLOCK
    query_ids = lax.axis_index("seq") * own_blocks + jnp.arange(own_blocks, dtype=jnp.int32)
    allowed = block_mask(
        query_ids, random_blocks[0], global_blocks[0], document_kv.shape[0] // BLOCK
    )
    attended = sparse_attention(query, keys, values, allowed, BLOCK)
    out_columns = out_weight[0]
    added = jnp.dot(
        lax.all_gather(attended, "dp", axis=1, tiled=True),
        out_columns,
        preferred_element_type=jnp.float32,
    )
    result = (token_rows.astype(jnp.float32) + added).astype(jnp.bfloat16)
    return shifted(result[None], "section", 1)


CHUNKS = 4


def relay_kernel(
    nz,
    x_ref,
    gain_ref,
    w_ref,
    ow_ref,
    rand_ref,
    glob_ref,
    out_ref,
    x_all,
    w_all,
    g_all,
    acc,
    q_s,
    kv,
    bias,
    m_s,
    l_s,
    o_s,
    att_own,
    att_all,
    x_next,
    ow_next,
    w_far,
    part_out,
    part_in,
    ss_out,
    ss_in,
    total_s,
    xs,
    xr,
    ws,
    wr,
    gs,
    gr,
    ks,
    kr,
    ts,
    tr,
    as_,
    ar,
    ns,
    nr,
    fs,
    fr,
    ps,
    pr,
    local,
):
    sec, p, y = lax.axis_index("section"), lax.axis_index("dp"), lax.axis_index("seq")
    dp = 2 * nz
    z, core = p // 2, p % 2
    sib = p + 1 - 2 * core
    tokens, feats = x_ref.shape
    width = feats * dp
    rows = tokens // CHUNKS
    head = q_s.shape[1]
    half = dp // 2
    scale = math.log2(math.e) / math.sqrt(head)

    barrier = pltpu.get_barrier_semaphore()
    for step in range(1, dp):
        pl.semaphore_signal(
            barrier, inc=1, device_id={"dp": lax.rem(p + step, dp)},
            device_id_type=pl.DeviceIdType.MESH,
        )
    for name, at in (("seq", 1 - y), ("section", 1 - sec)):
        pl.semaphore_signal(
            barrier, inc=1, device_id={name: at}, device_id_type=pl.DeviceIdType.MESH
        )

    def remote(src, dst, send, recv, where):
        return pltpu.make_async_remote_copy(
            src_ref=src, dst_ref=dst, send_sem=send, recv_sem=recv,
            device_id=where, device_id_type=pl.DeviceIdType.MESH,
        )

    def part(k):
        return pl.ds(k * rows, rows)

    def chunk(k):
        return pl.ds(pl.multiple_of(k * rows, rows), rows)

    own_x = pltpu.make_async_copy(x_ref, x_all.at[p], local.at[0])
    own_w = pltpu.make_async_copy(
        w_ref, w_all.at[pl.ds(pl.multiple_of(y * half * feats, feats), half * feats), :], local.at[1]
    )
    own_x.start()
    own_w.start()
    g_all[p] = jnp.broadcast_to(gain_ref[...].astype(jnp.float32), (8, feats))

    pl.semaphore_wait(barrier, dp + 1)

    def hop(buf, send, recv, way, b, k, src=None):
        at = buf.at[b, part(k), :]
        to = (p - 2, p + 2, sib)[way]
        return remote(at if src is None else src, at, send.at[way, b, k], recv.at[b, k], {"dp": to})

    def spread(buf, send, recv, b, k, ways, act, src=None):
        if 0 in ways:
            @pl.when(z > 0)
            def _():
                act(hop(buf, send, recv, 0, b, k, src))
        if 1 in ways:
            @pl.when(z < nz - 1)
            def _():
                act(hop(buf, send, recv, 1, b, k, src))
        act(hop(buf, send, recv, 2, b, k, src))

    start = lambda copy: copy.start()
    sent = lambda copy: copy.wait_send()

    def chain(buf, send, recv, d, k):
        @pl.when(z + d < nz)
        def _():
            b = p + 2 * d
            hop(buf, send, recv, 2, b, k).wait_recv()
            spread(buf, send, recv, b, k, (0,), start)

        @pl.when(z - d >= 0)
        def _():
            b = p - 2 * d
            hop(buf, send, recv, 2, b, k).wait_recv()
            spread(buf, send, recv, b, k, (1,), start)

    def drain(buf, send, recv, k, src=None):
        spread(buf, send, recv, p, k, (0, 1), sent, src)
        for d in range(1, nz):
            @pl.when(z + d < nz)
            def _():
                spread(buf, send, recv, p + 2 * d, k, (0,), sent)

            @pl.when(z - d >= 0)
            def _():
                spread(buf, send, recv, p - 2 * d, k, (1,), sent)

    near = z // (nz // 2)
    far = 1 - near
    inward = 2 - 4 * near
    is_end = (z == 0) | (z == nz - 1)
    is_helper = jnp.logical_not(is_end)
    in_far, in_near = y == far, y != far
    mate, end, far_end = p + inward, p - inward, p + 2 * inward

    def other(b):
        return b + 1 - 2 * core

    def xhop(way, b, k, own=False):
        at = x_all.at[b, part(k), :]
        to = (p + inward, p - inward, sib)[way]
        src = x_ref.at[part(k), :] if own else at
        return remote(src, at, xs.at[way, b, k], xr.at[b, k], {"dp": to})

    def arrived(b, k, *ways):
        xhop(2, b, k).wait_recv()
        for way in ways:
            xhop(way, b, k).start()

    def rows_of(j):
        return pl.ds(pl.multiple_of(j * feats, feats), feats)

    def w_copy(j):
        return remote(
            w_ref.at[rows_of(j), :], w_all.at[rows_of(y * half + j), :], ws.at[j], wr.at[j],
            {"seq": 1 - y},
        )

    def far_copy(j, src, where):
        return remote(src, w_far.at[rows_of(j), :], fs.at[j], fr.at[j], where)

    def far_from_end(j):
        return far_copy(j, w_ref.at[rows_of(j), :], {"dp": mate})

    def far_passed(j):
        return far_copy(j, w_all.at[rows_of(far * half + j), :], {"dp": mate})

    def far_shared(j):
        return far_copy(j, w_far.at[rows_of(j), :], {"seq": 1 - y})

    def gain_copy(to, src):
        return remote(g_all.at[src], g_all.at[src], gs.at[to], gr.at[src], {"dp": to})

    quarter = half // 2
    first_w = (1 - y) * quarter
    rest_w = y * quarter

    @pl.when(is_helper)
    def _():
        for k in range(CHUNKS):
            for way in (0, 1, 2):
                xhop(way, p, k, True).start()
        for j in range(quarter):
            w_copy(first_w + j).start()

    @pl.when(is_end & in_far)
    def _():
        for j in range(quarter):
            far_from_end(j).start()
            w_copy(quarter + j).start()
        for k in range(CHUNKS):
            xhop(0, p, k, True).start()
            xhop(2, p, k, True).start()

    @pl.when(is_end & in_near)
    def _():
        for k in range(CHUNKS // 2):
            xhop(0, p, k, True).start()
        for k in range(CHUNKS):
            xhop(2, p, k, True).start()
        for j in range(half):
            w_copy(j).start()

    for step in range(1, dp):
        gain_copy(lax.rem(p + step, dp), p).start()

    next_x = remote(x_ref, x_next, ns.at[0], nr.at[0], {"section": 1 - sec})
    next_w = remote(ow_ref, ow_next, ns.at[1], nr.at[1], {"section": 1 - sec})
    next_x.start()
    next_w.start()

    acc[...] = jnp.zeros_like(acc)

    blocks = tokens // BLOCK
    for h in range(2):
        key_at = y if h == 0 else 1 - y
        lane = lax.broadcasted_iota(jnp.int32, (blocks, tokens), 1)
        key_id = lane // BLOCK + key_at * blocks
        query_id = lax.broadcasted_iota(jnp.int32, (blocks, tokens), 0) + y * blocks
        allowed = jnp.abs(query_id - key_id) <= 1
        for g in range(glob_ref.shape[1]):
            number = glob_ref[:, g : g + 1]
            allowed = allowed | (key_id == number) | (query_id == number)
        for r in range(rand_ref.shape[1]):
            allowed = allowed | (key_id == rand_ref[:, r : r + 1])
        bias[h] = jnp.where(allowed, 0.0, -jnp.inf)

    def scaled(b, k):
        return (x_all[b, chunk(k), :].astype(jnp.float32) * g_all[b, 0:1, :]).astype(jnp.bfloat16)

    def project(b, k):
        acc[chunk(k), :] += jnp.dot(
            scaled(b, k), w_all[rows_of(b), :], preferred_element_type=jnp.float32
        )

    def project_whole(b):
        def body(k, _):
            project(b, k)
            return 0

        lax.fori_loop(0, CHUNKS, body, 0)

    def from_sib(b, k):
        xhop(2, b, k).wait_recv()

    def kv_copy(k):
        return remote(kv.at[0, part(k), :], kv.at[1, part(k), :], ks.at[k], kr.at[k], {"seq": 1 - y})

    def finish_joined(k, joined, total):
        joined = joined * lax.rsqrt(total / width + 1e-05)
        q_s[part(k), :] = joined[:, :head].astype(jnp.bfloat16)
        kv[0, part(k), :] = joined[:, head:].astype(jnp.bfloat16)
        kv_copy(k).start()

    def part_copies(k):
        return (
            remote(part_out.at[part(k), :], part_in.at[part(k), :], ps.at[0, k], pr.at[0, k], {"dp": end}),
            remote(ss_out.at[k], ss_in.at[k], ps.at[1, k], pr.at[1, k], {"dp": end}),
        )

    def diagonal():
        return lax.broadcasted_iota(jnp.int32, (rows, rows), 0) == lax.broadcasted_iota(
            jnp.int32, (rows, rows), 1
        )

    def help_end(k):
        if k == 0:
            @pl.when(in_far)
            def _():
                for j in range(quarter, half):
                    far_shared(j).wait_recv()

            @pl.when(in_near)
            def _():
                for j in range(quarter):
                    far_shared(j).wait_recv()

        from_sib(other(end), k)
        from_sib(other(far_end), k)
        part_sum = jnp.zeros((rows, acc.shape[1]), jnp.float32)
        for j in range(half):
            part_sum += jnp.dot(
                scaled(far * half + j, k), w_far[pl.ds(j * feats, feats), :],
                preferred_element_type=jnp.float32,
            )
        part_out[part(k), :] = part_sum.astype(jnp.bfloat16)
        folded = jnp.zeros((rows, 128), jnp.float32)
        for b in range(dp):
            for c in range(feats // 128):
                xb = x_all[b, part(k), c * 128 : (c + 1) * 128].astype(jnp.float32)
                folded += xb * xb
        total = jnp.sum(folded, axis=1, keepdims=True)
        total_s[part(k), :] = total
        across = jnp.sum(
            jnp.where(diagonal(), jnp.broadcast_to(total, (rows, rows)), 0.0), axis=0, keepdims=True
        )
        ss_out[k] = jnp.broadcast_to(across, (8, rows))
        for copy in part_copies(k):
            copy.start()

    def all_gains():
        for step in range(1, dp):
            gain_copy(sib, lax.rem(p + step, dp)).wait_recv()

    @pl.when(is_end)
    def _():
        @pl.when(in_near)
        def _():
            for j in range(quarter):
                w_copy(quarter + j).wait_recv()
                far_passed(quarter + j).start()
                for k in range(CHUNKS // 2 + j, CHUNKS, quarter):
                    xhop(0, p, k, True).start()

        for k in range(CHUNKS):
            arrived(mate, k, 2)
        own_x.wait()
        own_w.wait()
        all_gains()

        @pl.when(in_far)
        def _():
            for j in range(half):
                w_copy(j).wait_recv()

        for k in range(CHUNKS):
            from_sib(sib, k)
            from_sib(other(mate), k)
        for b in (p, sib, mate, other(mate)):
            project_whole(b)
        for k in range(CHUNKS):
            for copy in part_copies(k):
                copy.wait_recv()
            total = jnp.sum(
                jnp.where(diagonal(), jnp.broadcast_to(ss_in[k, 0:1, :], (rows, rows)), 0.0),
                axis=1, keepdims=True,
            )
            finish_joined(k, acc[part(k), :] + part_in[part(k), :].astype(jnp.float32), total)

    @pl.when(is_helper)
    def _():
        def share(j):
            far_shared(j).wait_recv()
            far_shared(j).start()

        def rest_of_w():
            for j in range(quarter):
                w_copy(rest_w + j).start()

        @pl.when(in_far)
        def _():
            arrived(mate, 0, 2)
            share(0)
            arrived(mate, 1, 2)
            arrived(mate, 2, 2)
            share(1)
            rest_of_w()
            arrived(mate, 3, 2)
            arrived(end, 0, 0, 2)
            arrived(end, 1, 0, 2)

        @pl.when(in_near)
        def _():
            arrived(mate, 0, 2)
            arrived(end, 0, 0, 2)
            arrived(mate, 1, 2)
            arrived(end, 1, 0, 2)
            arrived(mate, 2, 2)
            share(2)
            arrived(mate, 3, 2)
            rest_of_w()
            arrived(end, 2, 0, 2)
            share(3)

        own_x.wait()
        own_w.wait()
        all_gains()
        for j in range(quarter):
            w_copy(rest_w + j).wait_recv()
        for k in range(CHUNKS):
            from_sib(sib, k)
            from_sib(other(mate), k)
        for b in (p, sib, mate, other(mate)):
            project_whole(b)

        held = jnp.where(near == y, end, far_end)
        missing = jnp.where(near == y, far_end, end)

        def help_and_project(k):
            help_end(k)
            project(held, k)
            project(other(held), k)

        for k in range(CHUNKS):
            if k == 2:
                @pl.when(in_far)
                def _():
                    arrived(end, 2, 0, 2)

            if k == 3:
                arrived(end, 3, 0, 2)
            arrived(far_end, k, 2)
            if k > 0:
                help_and_project(k - 1)
        help_and_project(CHUNKS - 1)
        for j in range(quarter):
            w_copy(first_w + j).wait_recv()
        for k in range(CHUNKS):
            project(missing, k)
            project(other(missing), k)
            finish_joined(k, acc[part(k), :], total_s[part(k), :])

    per = blocks // CHUNKS

    def scores_of(k, h):
        s = lax.dot_general(
            q_s[part(k), :], kv[h, :, :head], (((1,), (1,)), ((), ())),
            preferred_element_type=jnp.float32,
        )
        s = (s * scale).reshape(per, BLOCK, tokens)
        s = s + bias[h, k * per : (k + 1) * per, :][:, None, :]
        return s.reshape(rows, tokens)

    def own_keys(k):
        s = scores_of(k, 0)
        m = jnp.max(s, axis=1, keepdims=True)
        e = jnp.exp2(s - m)
        m_s[part(k), :] = m
        l_s[part(k), :] = jnp.sum(e, axis=1, keepdims=True)
        o_s[part(k), :] = jnp.dot(
            e.astype(jnp.bfloat16), kv[0, :, head:], preferred_element_type=jnp.float32
        )

    def att_copy(k):
        return remote(
            att_own.at[part(k), :], att_all.at[p, part(k), :], ts.at[k], ar.at[p, k], {"section": 1 - sec}
        )

    def other_keys(k):
        s = scores_of(k, 1)
        before = m_s[part(k), :]
        m = jnp.maximum(before, jnp.max(s, axis=1, keepdims=True))
        e = jnp.exp2(s - m)
        shrink = jnp.exp2(before - m)
        total = l_s[part(k), :] * shrink + jnp.sum(e, axis=1, keepdims=True)
        o = o_s[part(k), :] * shrink + jnp.dot(
            e.astype(jnp.bfloat16), kv[1, :, head:], preferred_element_type=jnp.float32
        )
        att_own[part(k), :] = (o / total).astype(jnp.bfloat16)
        att_copy(k).start()

    for k in range(CHUNKS):
        own_keys(k)
    for k in range(CHUNKS):
        kv_copy(k).wait_recv()
    next_x.wait_recv()
    next_w.wait_recv()

    def att_step(d, k):
        if d == 0:
            att_copy(k).wait_recv()
            spread(att_all, as_, ar, p, k, (0, 1), start)
        else:
            chain(att_all, as_, ar, d, k)

    def finish(k):
        hop(att_all, as_, ar, 2, sib, k).wait_recv()
        for d in range(1, nz):
            @pl.when(z + d < nz)
            def _():
                hop(att_all, as_, ar, 2, sib + 2 * d, k).wait_recv()

            @pl.when(z - d >= 0)
            def _():
                hop(att_all, as_, ar, 2, sib - 2 * d, k).wait_recv()
        heads = jnp.concatenate([att_all[b, part(k), :] for b in range(dp)], axis=1)
        added = jnp.dot(heads, ow_next[...], preferred_element_type=jnp.float32)
        out_ref[part(k), :] = (x_next[part(k), :].astype(jnp.float32) + added).astype(jnp.bfloat16)

    for i in range(CHUNKS + nz + 1):
        if i < CHUNKS:
            other_keys(i)
        for d in range(nz):
            if 0 <= i - 1 - d < CHUNKS:
                att_step(d, i - 1 - d)
        if 0 <= i - nz - 1 < CHUNKS:
            finish(i - nz - 1)

    for k in range(CHUNKS):
        drain(att_all, as_, ar, k)
        kv_copy(k).wait_send()
        att_copy(k).wait_send()
        xhop(2, p, k, True).wait_send()
        xhop(0, p, k, True).wait_send()
        xhop(2, mate, k).wait_send()

        @pl.when(is_helper)
        def _():
            xhop(1, p, k, True).wait_send()
            xhop(0, end, k).wait_send()
            xhop(2, end, k).wait_send()
            xhop(2, far_end, k).wait_send()
            for copy in part_copies(k):
                copy.wait_send()

    for step in range(1, dp):
        gain_copy(lax.rem(p + step, dp), p).wait_send()
    for j in range(quarter):
        w_copy(quarter + j).wait_send()

        @pl.when(jnp.logical_not(is_end & in_far))
        def _():
            w_copy(j).wait_send()

        @pl.when(in_far)
        def _():
            far_shared(j).wait_send()

        @pl.when(in_near)
        def _():
            far_shared(quarter + j).wait_send()

    next_x.wait_send()
    next_w.wait_send()


def relay(dp, x, gain, w, ow, rand, glob):
    nz = dp // 2
    tokens, feats = x.shape
    columns = w.shape[1]
    head = columns // 3
    vmem = pl.BlockSpec(memory_space=pltpu.VMEM)
    anywhere = pl.BlockSpec(memory_space=pl.ANY)
    bf16, f32, dma = jnp.bfloat16, jnp.float32, pltpu.SemaphoreType.DMA
    return pl.pallas_call(
        functools.partial(relay_kernel, nz),
        out_shape=jax.ShapeDtypeStruct((tokens, feats), bf16),
        in_specs=[anywhere, vmem, anywhere, anywhere, vmem, vmem],
        out_specs=vmem,
        scratch_shapes=[
            pltpu.VMEM((dp, tokens, feats), bf16),
            pltpu.VMEM((dp * feats, columns), bf16),
            pltpu.VMEM((dp, 8, feats), f32),
            pltpu.VMEM((tokens, columns), f32),
            pltpu.VMEM((tokens, head), bf16),
            pltpu.VMEM((2, tokens, 2 * head), bf16),
            pltpu.VMEM((2, tokens // BLOCK, tokens), f32),
            pltpu.VMEM((tokens, 1), f32),
            pltpu.VMEM((tokens, 1), f32),
            pltpu.VMEM((tokens, head), f32),
            pltpu.VMEM((tokens, head), bf16),
            pltpu.VMEM((dp, tokens, head), bf16),
            pltpu.VMEM((tokens, feats), bf16),
            pltpu.VMEM(ow.shape, bf16),
            pltpu.VMEM((dp // 2 * feats, columns), bf16),
            pltpu.VMEM((tokens, columns), bf16),
            pltpu.VMEM((tokens, columns), bf16),
            pltpu.VMEM((CHUNKS, 8, tokens // CHUNKS), f32),
            pltpu.VMEM((CHUNKS, 8, tokens // CHUNKS), f32),
            pltpu.VMEM((tokens, 1), f32),
            dma((3, dp, CHUNKS)),
            dma((dp, CHUNKS)),
            dma((dp // 2,)),
            dma((dp // 2,)),
            dma((dp,)),
            dma((dp,)),
            dma((CHUNKS,)),
            dma((CHUNKS,)),
            dma((CHUNKS,)),
            dma((CHUNKS,)),
            dma((3, dp, CHUNKS)),
            dma((dp, CHUNKS)),
            dma((2,)),
            dma((2,)),
            dma((dp // 2,)),
            dma((dp // 2,)),
            dma((2, CHUNKS)),
            dma((2, CHUNKS)),
            dma((2,)),
        ],
        compiler_params=pltpu.CompilerParams(
            collective_id=0, has_side_effects=True, vmem_limit_bytes=56 * 1024 * 1024
        ),
        name="relay_layer",
    )(x, gain, w, ow, rand, glob)


def tiles(mesh, tokens, feats, columns):
    return (
        mesh.shape["section"] == 2
        and mesh.shape["seq"] == 2
        and mesh.shape["dp"] == 8
        and feats % 128 == 0
        and columns % 384 == 0
        and tokens % (CHUNKS * BLOCK) == 0
    )


def solution(mesh):
    placed = (
        P("section", "seq", "dp"),
        P("section", "dp"),
        P("section", "seq", "dp"),
        P("section", None, "dp"),
        P("section", "seq", None),
        P("section", None),
    )

    def layer(section_input, norm_gain, qkv_weight, out_weight, random_blocks, global_blocks):
        args = (section_input, norm_gain, qkv_weight, out_weight, random_blocks, global_blocks)
        _, tokens, feats = section_input.shape
        if not tiles(mesh, tokens, feats, qkv_weight.shape[2]):
            return shards(*args)
        out = relay(
            mesh.shape["dp"], section_input[0], norm_gain, qkv_weight[0], out_weight[0],
            random_blocks[0], global_blocks,
        )
        return out[None]

    return jax.shard_map(
        layer, mesh=mesh, in_specs=placed, out_specs=P("section", "seq", "dp"), check_vma=False
    )
```

```python
import functools
import math

import jax
import jax.numpy as jnp
from jax import lax
from jax.experimental import pallas as pl
from jax.experimental.pallas import tpu as pltpu
from jax.sharding import PartitionSpec as P

BLOCK = 64


def shifted(block, axis, distance):
    devices = range(lax.axis_size(axis))
    route = [((i - distance) % len(devices), i) for i in devices]
    return lax.ppermute(block, axis, route)


def block_mask(query_ids, random_rows, global_ids, key_count):
    query_col = query_ids[:, None]
    key_ids = jnp.arange(key_count, dtype=jnp.int32)[None, :]
    adjacent = jnp.abs(query_col - key_ids) <= 1
    key_global = jnp.any(key_ids[:, :, None] == global_ids[None, None, :], axis=2)
    query_global = jnp.any(query_col[:, :, None] == global_ids[None, None, :], axis=2)
    chosen = jnp.any(random_rows[:, None, :] == key_ids[:, :, None], axis=2)
    return adjacent | key_global | query_global | chosen


def sparse_attention(query, keys, values, allowed, block_size):
    scores = lax.dot_general(
        query, keys, (((1,), (1,)), ((), ())), preferred_element_type=jnp.float32
    )
    scores = scores * (1.0 / math.sqrt(query.shape[1]))
    query_blocks, key_blocks = allowed.shape
    scores = scores.reshape(query_blocks, block_size, key_blocks, block_size)
    live = allowed[:, None, :, None]
    scores = jnp.where(live, scores, -1e30)
    highest = jnp.max(scores, axis=(2, 3), keepdims=True)
    weights = jnp.where(live, jnp.exp(scores - highest), 0.0)
    totals = jnp.sum(weights, axis=(2, 3), keepdims=True)
    probs = (
        (weights / totals)
        .reshape(query_blocks * block_size, key_blocks * block_size)
        .astype(jnp.bfloat16)
    )
    return jnp.dot(probs, values, preferred_element_type=jnp.float32).astype(jnp.bfloat16)


def shards(section_input, norm_gain, qkv_weight, out_weight, random_blocks, global_blocks):
    token_rows = section_input[0]
    token_count = token_rows.shape[0]
    width = norm_gain.shape[1] * lax.axis_size("dp")
    as_float = token_rows.astype(jnp.float32)
    local_squares = jnp.sum(as_float * as_float, axis=1)
    total_squares = lax.psum(local_squares, "dp")
    factor = lax.rsqrt(total_squares / width + 1e-05)[:, None]
    normed_part = (as_float * factor * norm_gain[0].astype(jnp.float32)).astype(jnp.bfloat16)
    normed = lax.all_gather(normed_part, "dp", axis=1, tiled=True)
    weight_half = qkv_weight[0]
    joined = jnp.dot(
        normed,
        lax.all_gather(weight_half, "seq", axis=0, tiled=True),
        preferred_element_type=jnp.float32,
    )
    head_size = joined.shape[1] // 3
    query = joined[:, :head_size].astype(jnp.bfloat16)
    keys_values = joined[:, head_size:].astype(jnp.bfloat16)
    document_kv = lax.all_gather(keys_values, "seq", axis=0, tiled=True)
    keys = document_kv[:, :head_size]
    values = document_kv[:, head_size:]
    own_blocks = token_count // BLOCK
    query_ids = lax.axis_index("seq") * own_blocks + jnp.arange(own_blocks, dtype=jnp.int32)
    allowed = block_mask(
        query_ids, random_blocks[0], global_blocks[0], document_kv.shape[0] // BLOCK
    )
    attended = sparse_attention(query, keys, values, allowed, BLOCK)
    out_columns = out_weight[0]
    added = jnp.dot(
        lax.all_gather(attended, "dp", axis=1, tiled=True),
        out_columns,
        preferred_element_type=jnp.float32,
    )
    result = (token_rows.astype(jnp.float32) + added).astype(jnp.bfloat16)
    return shifted(result[None], "section", 1)


CHUNKS = 4


def relay_kernel(
    nz,
    x_ref,
    gain_ref,
    w_ref,
    ow_ref,
    rand_ref,
    glob_ref,
    out_ref,
    x_all,
    w_all,
    g_all,
    acc,
    q_s,
    kv,
    bias,
    m_s,
    l_s,
    o_s,
    att_own,
    att_all,
    x_next,
    ow_next,
    w_far,
    part_out,
    part_in,
    ss_out,
    ss_in,
    total_s,
    rand_s,
    xs,
    xr,
    ws,
    wr,
    gs,
    gr,
    ks,
    kr,
    ts,
    tr,
    as_,
    ar,
    ns,
    nr,
    fs,
    fr,
    ps,
    pr,
    local,
):
    sec, p, y = lax.axis_index("section"), lax.axis_index("dp"), lax.axis_index("seq")
    dp = 2 * nz
    z, core = p // 2, p % 2
    sib = p + 1 - 2 * core
    tokens, feats = x_ref.shape
    width = feats * dp
    rows = tokens // CHUNKS
    head = q_s.shape[1]
    half = dp // 2
    scale = math.log2(math.e) / math.sqrt(head)

    barrier = pltpu.get_barrier_semaphore()
    for step in range(1, dp):
        pl.semaphore_signal(
            barrier, inc=1, device_id={"dp": lax.rem(p + step, dp)},
            device_id_type=pl.DeviceIdType.MESH,
        )
    for name, at in (("seq", 1 - y), ("section", 1 - sec)):
        pl.semaphore_signal(
            barrier, inc=1, device_id={name: at}, device_id_type=pl.DeviceIdType.MESH
        )

    def remote(src, dst, send, recv, where):
        return pltpu.make_async_remote_copy(
            src_ref=src, dst_ref=dst, send_sem=send, recv_sem=recv,
            device_id=where, device_id_type=pl.DeviceIdType.MESH,
        )

    def part(k):
        return pl.ds(k * rows, rows)

    def chunk(k):
        return pl.ds(pl.multiple_of(k * rows, rows), rows)

    own_x = pltpu.make_async_copy(x_ref, x_all.at[p], local.at[0])
    own_w = pltpu.make_async_copy(
        w_ref, w_all.at[pl.ds(pl.multiple_of(y * half * feats, feats), half * feats), :], local.at[1]
    )
    rand_copy = pltpu.make_async_copy(rand_ref, rand_s, local.at[2])
    rand_copy.start()
    own_x.start()
    own_w.start()
    g_all[p] = jnp.broadcast_to(gain_ref[...].astype(jnp.float32), (8, feats))

    pl.semaphore_wait(barrier, dp + 1)

    def hop(buf, send, recv, way, b, k, src=None):
        at = buf.at[b, part(k), :]
        to = (p - 2, p + 2, sib)[way]
        return remote(at if src is None else src, at, send.at[way, b, k], recv.at[b, k], {"dp": to})

    def spread(buf, send, recv, b, k, ways, act, src=None):
        if 0 in ways:
            @pl.when(z > 0)
            def _():
                act(hop(buf, send, recv, 0, b, k, src))
        if 1 in ways:
            @pl.when(z < nz - 1)
            def _():
                act(hop(buf, send, recv, 1, b, k, src))
        act(hop(buf, send, recv, 2, b, k, src))

    start = lambda copy: copy.start()
    sent = lambda copy: copy.wait_send()

    def chain(buf, send, recv, d, k):
        @pl.when(z + d < nz)
        def _():
            b = p + 2 * d
            hop(buf, send, recv, 2, b, k).wait_recv()
            spread(buf, send, recv, b, k, (0,), start)

        @pl.when(z - d >= 0)
        def _():
            b = p - 2 * d
            hop(buf, send, recv, 2, b, k).wait_recv()
            spread(buf, send, recv, b, k, (1,), start)

    def drain(buf, send, recv, k, src=None):
        spread(buf, send, recv, p, k, (0, 1), sent, src)
        for d in range(1, nz):
            @pl.when(z + d < nz)
            def _():
                spread(buf, send, recv, p + 2 * d, k, (0,), sent)

            @pl.when(z - d >= 0)
            def _():
                spread(buf, send, recv, p - 2 * d, k, (1,), sent)

    near = z // (nz // 2)
    far = 1 - near
    inward = 2 - 4 * near
    is_end = (z == 0) | (z == nz - 1)
    is_helper = jnp.logical_not(is_end)
    in_far, in_near = y == far, y != far
    mate, end, far_end = p + inward, p - inward, p + 2 * inward

    def other(b):
        return b + 1 - 2 * core

    def xhop(way, b, k, own=False):
        at = x_all.at[b, part(k), :]
        to = (p + inward, p - inward, sib)[way]
        src = x_ref.at[part(k), :] if own else at
        return remote(src, at, xs.at[way, b, k], xr.at[b, k], {"dp": to})

    def arrived(b, k, *ways):
        xhop(2, b, k).wait_recv()
        for way in ways:
            xhop(way, b, k).start()

    def rows_of(j):
        return pl.ds(pl.multiple_of(j * feats, feats), feats)

    def w_copy(j):
        return remote(
            w_ref.at[rows_of(j), :], w_all.at[rows_of(y * half + j), :], ws.at[j], wr.at[j],
            {"seq": 1 - y},
        )

    def far_copy(j, src, where):
        return remote(src, w_far.at[rows_of(j), :], fs.at[j], fr.at[j], where)

    def far_from_end(j):
        return far_copy(j, w_ref.at[rows_of(j), :], {"dp": mate})

    def far_passed(j):
        return far_copy(j, w_all.at[rows_of(far * half + j), :], {"dp": mate})

    def far_shared(j):
        return far_copy(j, w_far.at[rows_of(j), :], {"seq": 1 - y})

    def gain_copy(to, src):
        return remote(g_all.at[src], g_all.at[src], gs.at[to], gr.at[src], {"dp": to})

    quarter = half // 2
    first_w = (1 - y) * quarter
    rest_w = y * quarter

    @pl.when(is_helper)
    def _():
        for k in range(CHUNKS):
            for way in (0, 1, 2):
                xhop(way, p, k, True).start()
        for j in range(quarter):
            w_copy(first_w + j).start()

    @pl.when(is_end & in_far)
    def _():
        for j in range(quarter):
            far_from_end(j).start()
            w_copy(quarter + j).start()
        for k in range(CHUNKS):
            xhop(2, p, k, True).start()

    @pl.when(is_end & in_near)
    def _():
        for k in range(CHUNKS // 2):
            xhop(0, p, k, True).start()
        for k in range(CHUNKS):
            xhop(2, p, k, True).start()
        for j in range(half):
            w_copy(j).start()

    for step in range(1, dp):
        gain_copy(lax.rem(p + step, dp), p).start()

    next_x = remote(x_ref, x_next, ns.at[0], nr.at[0], {"section": 1 - sec})
    next_w = remote(ow_ref, ow_next, ns.at[1], nr.at[1], {"section": 1 - sec})
    next_x.start()
    next_w.start()

    acc[...] = jnp.zeros_like(acc)

    rand_copy.wait()

    blocks = tokens // BLOCK
    for h in range(2):
        key_at = y if h == 0 else 1 - y
        lane = lax.broadcasted_iota(jnp.int32, (blocks, tokens), 1)
        key_id = lane // BLOCK + key_at * blocks
        query_id = lax.broadcasted_iota(jnp.int32, (blocks, tokens), 0) + y * blocks
        allowed = jnp.abs(query_id - key_id) <= 1
        for g in range(glob_ref.shape[1]):
            number = glob_ref[:, g : g + 1]
            allowed = allowed | (key_id == number) | (query_id == number)
        for r in range(rand_ref.shape[2]):
            allowed = allowed | (key_id == rand_s[0, :, r : r + 1])
        bias[h] = jnp.where(allowed, 0.0, -jnp.inf)

    def scaled(b, k):
        return (x_all[b, chunk(k), :].astype(jnp.float32) * g_all[b, 0:1, :]).astype(jnp.bfloat16)

    def project(b, k):
        acc[chunk(k), :] += jnp.dot(
            scaled(b, k), w_all[rows_of(b), :], preferred_element_type=jnp.float32
        )

    def project_whole(b):
        def body(k, _):
            project(b, k)
            return 0

        lax.fori_loop(0, CHUNKS, body, 0)

    def from_sib(b, k):
        xhop(2, b, k).wait_recv()

    def kv_copy(k):
        return remote(kv.at[0, part(k), :], kv.at[1, part(k), :], ks.at[k], kr.at[k], {"seq": 1 - y})

    def finish_joined(k, joined, total):
        joined = joined * lax.rsqrt(total / width + 1e-05)
        q_s[part(k), :] = joined[:, :head].astype(jnp.bfloat16)
        kv[0, part(k), :] = joined[:, head:].astype(jnp.bfloat16)
        kv_copy(k).start()

    def part_copies(k):
        return (
            remote(part_out.at[part(k), :], part_in.at[part(k), :], ps.at[0, k], pr.at[0, k], {"dp": end}),
            remote(ss_out.at[k], ss_in.at[k], ps.at[1, k], pr.at[1, k], {"dp": end}),
        )

    def diagonal():
        return lax.broadcasted_iota(jnp.int32, (rows, rows), 0) == lax.broadcasted_iota(
            jnp.int32, (rows, rows), 1
        )

    def help_end(k):
        if k == 0:
            @pl.when(in_far)
            def _():
                for j in range(quarter, half):
                    far_shared(j).wait_recv()

            @pl.when(in_near)
            def _():
                for j in range(quarter):
                    far_shared(j).wait_recv()

        from_sib(other(end), k)
        from_sib(other(far_end), k)
        part_sum = jnp.zeros((rows, acc.shape[1]), jnp.float32)
        for j in range(half):
            part_sum += jnp.dot(
                scaled(far * half + j, k), w_far[pl.ds(j * feats, feats), :],
                preferred_element_type=jnp.float32,
            )
        part_out[part(k), :] = part_sum.astype(jnp.bfloat16)
        folded = jnp.zeros((rows, 128), jnp.float32)
        for b in range(dp):
            for c in range(feats // 128):
                xb = x_all[b, part(k), c * 128 : (c + 1) * 128].astype(jnp.float32)
                folded += xb * xb
        total = jnp.sum(folded, axis=1, keepdims=True)
        total_s[part(k), :] = total
        across = jnp.sum(
            jnp.where(diagonal(), jnp.broadcast_to(total, (rows, rows)), 0.0), axis=0, keepdims=True
        )
        ss_out[k] = jnp.broadcast_to(across, (8, rows))
        for copy in part_copies(k):
            copy.start()

    def all_gains():
        for step in range(1, dp):
            gain_copy(sib, lax.rem(p + step, dp)).wait_recv()

    @pl.when(is_end)
    def _():
        @pl.when(in_far)
        def _():
            for j in range(quarter):
                far_from_end(j).wait_send()
            for k in range(CHUNKS):
                xhop(0, p, k, True).start()

        @pl.when(in_near)
        def _():
            for j in range(quarter):
                w_copy(quarter + j).wait_recv()
                far_passed(quarter + j).start()
                for k in range(CHUNKS // 2 + j, CHUNKS, quarter):
                    xhop(0, p, k, True).start()

        for k in range(CHUNKS):
            arrived(mate, k, 2)
        own_x.wait()
        own_w.wait()
        all_gains()

        @pl.when(in_far)
        def _():
            for j in range(half):
                w_copy(j).wait_recv()

        for k in range(CHUNKS):
            from_sib(sib, k)
            from_sib(other(mate), k)
        for b in (p, sib, mate, other(mate)):
            project_whole(b)
        for k in range(CHUNKS):
            for copy in part_copies(k):
                copy.wait_recv()
            total = jnp.sum(
                jnp.where(diagonal(), jnp.broadcast_to(ss_in[k, 0:1, :], (rows, rows)), 0.0),
                axis=1, keepdims=True,
            )
            finish_joined(k, acc[part(k), :] + part_in[part(k), :].astype(jnp.float32), total)

    @pl.when(is_helper)
    def _():
        def share(j):
            far_shared(j).wait_recv()
            far_shared(j).start()

        def when_far(fn):
            pl.when(in_far)(fn)

        def when_near(fn):
            pl.when(in_near)(fn)

        arrived(mate, 0, 2)
        when_near(lambda: arrived(end, 0, 0, 2))
        when_far(lambda: share(0))
        arrived(mate, 1, 2)
        when_near(lambda: arrived(end, 1, 0, 2))
        arrived(mate, 2, 2)
        when_far(lambda: share(1))
        when_near(lambda: share(2))
        arrived(mate, 3, 2)
        when_far(lambda: arrived(end, 0, 0, 2))

        own_x.wait()
        own_w.wait()
        all_gains()
        for j in range(quarter):
            w_copy(rest_w + j).wait_recv()
        for k in range(CHUNKS):
            from_sib(sib, k)
            from_sib(other(mate), k)
        project_whole(p)
        project_whole(sib)
        when_far(lambda: arrived(end, 1, 0, 2))
        when_near(lambda: share(3))
        project_whole(mate)
        project_whole(other(mate))
        arrived(end, 2, 0, 2)

        @pl.when(in_far)
        def _():
            for j in range(quarter):
                far_shared(j).wait_send()

        @pl.when(in_near)
        def _():
            for j in range(quarter, half):
                far_shared(j).wait_send()

        for j in range(quarter):
            w_copy(rest_w + j).start()

        held = jnp.where(near == y, end, far_end)
        missing = jnp.where(near == y, far_end, end)

        def help_and_project(k):
            help_end(k)
            project(held, k)
            project(other(held), k)

        for k in range(CHUNKS):
            if k == 2:
                arrived(end, 3, 0, 2)
            arrived(far_end, k, 2)
            if k > 0:
                help_and_project(k - 1)
        help_and_project(CHUNKS - 1)
        for j in range(quarter):
            w_copy(first_w + j).wait_recv()
        for k in range(CHUNKS):
            project(missing, k)
            project(other(missing), k)
            finish_joined(k, acc[part(k), :], total_s[part(k), :])

    per = blocks // CHUNKS

    def scores_of(k, h):
        s = lax.dot_general(
            q_s[part(k), :], kv[h, :, :head], (((1,), (1,)), ((), ())),
            preferred_element_type=jnp.float32,
        )
        s = (s * scale).reshape(per, BLOCK, tokens)
        s = s + bias[h, k * per : (k + 1) * per, :][:, None, :]
        return s.reshape(rows, tokens)

    def own_keys(k):
        s = scores_of(k, 0)
        m = jnp.max(s, axis=1, keepdims=True)
        e = jnp.exp2(s - m)
        m_s[part(k), :] = m
        l_s[part(k), :] = jnp.sum(e, axis=1, keepdims=True)
        o_s[part(k), :] = jnp.dot(
            e.astype(jnp.bfloat16), kv[0, :, head:], preferred_element_type=jnp.float32
        )

    def att_copy(k):
        return remote(
            att_own.at[part(k), :], att_all.at[p, part(k), :], ts.at[k], ar.at[p, k], {"section": 1 - sec}
        )

    def other_keys(k):
        s = scores_of(k, 1)
        before = m_s[part(k), :]
        m = jnp.maximum(before, jnp.max(s, axis=1, keepdims=True))
        e = jnp.exp2(s - m)
        shrink = jnp.exp2(before - m)
        total = l_s[part(k), :] * shrink + jnp.sum(e, axis=1, keepdims=True)
        o = o_s[part(k), :] * shrink + jnp.dot(
            e.astype(jnp.bfloat16), kv[1, :, head:], preferred_element_type=jnp.float32
        )
        att_own[part(k), :] = (o / total).astype(jnp.bfloat16)
        att_copy(k).start()

    for k in range(CHUNKS):
        own_keys(k)
    for k in range(CHUNKS):
        kv_copy(k).wait_recv()
    next_x.wait_recv()
    next_w.wait_recv()

    def att_step(d, k):
        if d == 0:
            att_copy(k).wait_recv()
            spread(att_all, as_, ar, p, k, (0, 1), start)
        else:
            chain(att_all, as_, ar, d, k)

    def finish(k):
        hop(att_all, as_, ar, 2, sib, k).wait_recv()
        for d in range(1, nz):
            @pl.when(z + d < nz)
            def _():
                hop(att_all, as_, ar, 2, sib + 2 * d, k).wait_recv()

            @pl.when(z - d >= 0)
            def _():
                hop(att_all, as_, ar, 2, sib - 2 * d, k).wait_recv()
        heads = jnp.concatenate([att_all[b, part(k), :] for b in range(dp)], axis=1)
        added = jnp.dot(heads, ow_next[...], preferred_element_type=jnp.float32)
        out_ref[part(k), :] = (x_next[part(k), :].astype(jnp.float32) + added).astype(jnp.bfloat16)

    for i in range(CHUNKS + nz + 1):
        if i < CHUNKS:
            other_keys(i)
        for d in range(nz):
            if 0 <= i - 1 - d < CHUNKS:
                att_step(d, i - 1 - d)
        if 0 <= i - nz - 1 < CHUNKS:
            finish(i - nz - 1)

    for k in range(CHUNKS):
        drain(att_all, as_, ar, k)
        kv_copy(k).wait_send()
        att_copy(k).wait_send()
        xhop(2, p, k, True).wait_send()
        xhop(0, p, k, True).wait_send()
        xhop(2, mate, k).wait_send()

        @pl.when(is_helper)
        def _():
            xhop(1, p, k, True).wait_send()
            xhop(0, end, k).wait_send()
            xhop(2, end, k).wait_send()
            xhop(2, far_end, k).wait_send()
            for copy in part_copies(k):
                copy.wait_send()

    for step in range(1, dp):
        gain_copy(lax.rem(p + step, dp), p).wait_send()
    for j in range(quarter):
        w_copy(quarter + j).wait_send()

        @pl.when(jnp.logical_not(is_end & in_far))
        def _():
            w_copy(j).wait_send()

        @pl.when(is_end & in_near)
        def _():
            far_passed(quarter + j).wait_send()

    next_x.wait_send()
    next_w.wait_send()


def relay(dp, x, gain, w, ow, rand, glob):
    nz = dp // 2
    tokens, feats = x.shape
    columns = w.shape[1]
    head = columns // 3
    vmem = pl.BlockSpec(memory_space=pltpu.VMEM)
    anywhere = pl.BlockSpec(memory_space=pl.ANY)
    bf16, f32, dma = jnp.bfloat16, jnp.float32, pltpu.SemaphoreType.DMA
    return pl.pallas_call(
        functools.partial(relay_kernel, nz),
        out_shape=jax.ShapeDtypeStruct((tokens, feats), bf16),
        in_specs=[anywhere, vmem, anywhere, anywhere, anywhere, vmem],
        out_specs=vmem,
        scratch_shapes=[
            pltpu.VMEM((dp, tokens, feats), bf16),
            pltpu.VMEM((dp * feats, columns), bf16),
            pltpu.VMEM((dp, 8, feats), f32),
            pltpu.VMEM((tokens, columns), f32),
            pltpu.VMEM((tokens, head), bf16),
            pltpu.VMEM((2, tokens, 2 * head), bf16),
            pltpu.VMEM((2, tokens // BLOCK, tokens), f32),
            pltpu.VMEM((tokens, 1), f32),
            pltpu.VMEM((tokens, 1), f32),
            pltpu.VMEM((tokens, head), f32),
            pltpu.VMEM((tokens, head), bf16),
            pltpu.VMEM((dp, tokens, head), bf16),
            pltpu.VMEM((tokens, feats), bf16),
            pltpu.VMEM(ow.shape, bf16),
            pltpu.VMEM((dp // 2 * feats, columns), bf16),
            pltpu.VMEM((tokens, columns), bf16),
            pltpu.VMEM((tokens, columns), bf16),
            pltpu.VMEM((CHUNKS, 8, tokens // CHUNKS), f32),
            pltpu.VMEM((CHUNKS, 8, tokens // CHUNKS), f32),
            pltpu.VMEM((tokens, 1), f32),
            pltpu.VMEM(rand.shape, jnp.int32),
            dma((3, dp, CHUNKS)),
            dma((dp, CHUNKS)),
            dma((dp // 2,)),
            dma((dp // 2,)),
            dma((dp,)),
            dma((dp,)),
            dma((CHUNKS,)),
            dma((CHUNKS,)),
            dma((CHUNKS,)),
            dma((CHUNKS,)),
            dma((3, dp, CHUNKS)),
            dma((dp, CHUNKS)),
            dma((2,)),
            dma((2,)),
            dma((dp // 2,)),
            dma((dp // 2,)),
            dma((2, CHUNKS)),
            dma((2, CHUNKS)),
            dma((3,)),
        ],
        compiler_params=pltpu.CompilerParams(
            collective_id=0, has_side_effects=True, vmem_limit_bytes=56 * 1024 * 1024
        ),
        name="relay_layer",
    )(x, gain, w, ow, rand, glob)


def tiles(mesh, tokens, feats, columns):
    return (
        mesh.shape["section"] == 2
        and mesh.shape["seq"] == 2
        and mesh.shape["dp"] == 8
        and feats % 128 == 0
        and columns % 384 == 0
        and tokens % (CHUNKS * BLOCK) == 0
    )


def solution(mesh):
    placed = (
        P("section", "seq", "dp"),
        P("section", "dp"),
        P("section", "seq", "dp"),
        P("section", None, "dp"),
        P("section", "seq", None),
        P("section", None),
    )

    def layer(section_input, norm_gain, qkv_weight, out_weight, random_blocks, global_blocks):
        args = (section_input, norm_gain, qkv_weight, out_weight, random_blocks, global_blocks)
        _, tokens, feats = section_input.shape
        if not tiles(mesh, tokens, feats, qkv_weight.shape[2]):
            return shards(*args)
        out = relay(
            mesh.shape["dp"], section_input[0], norm_gain, qkv_weight[0], out_weight[0],
            random_blocks, global_blocks,
        )
        return out[None]

    return jax.shard_map(
        layer, mesh=mesh, in_specs=placed, out_specs=P("section", "seq", "dp"), check_vma=False
    )
```

```python
import functools
import math

import jax
import jax.numpy as jnp
from jax import lax
from jax.experimental import pallas as pl
from jax.experimental.pallas import tpu as pltpu
from jax.sharding import PartitionSpec as P

BLOCK = 64


def shifted(block, axis, distance):
    devices = range(lax.axis_size(axis))
    route = [((i - distance) % len(devices), i) for i in devices]
    return lax.ppermute(block, axis, route)


def block_mask(query_ids, random_rows, global_ids, key_count):
    query_col = query_ids[:, None]
    key_ids = jnp.arange(key_count, dtype=jnp.int32)[None, :]
    adjacent = jnp.abs(query_col - key_ids) <= 1
    key_global = jnp.any(key_ids[:, :, None] == global_ids[None, None, :], axis=2)
    query_global = jnp.any(query_col[:, :, None] == global_ids[None, None, :], axis=2)
    chosen = jnp.any(random_rows[:, None, :] == key_ids[:, :, None], axis=2)
    return adjacent | key_global | query_global | chosen


def sparse_attention(query, keys, values, allowed, block_size):
    scores = lax.dot_general(
        query, keys, (((1,), (1,)), ((), ())), preferred_element_type=jnp.float32
    )
    scores = scores * (1.0 / math.sqrt(query.shape[1]))
    query_blocks, key_blocks = allowed.shape
    scores = scores.reshape(query_blocks, block_size, key_blocks, block_size)
    live = allowed[:, None, :, None]
    scores = jnp.where(live, scores, -1e30)
    highest = jnp.max(scores, axis=(2, 3), keepdims=True)
    weights = jnp.where(live, jnp.exp(scores - highest), 0.0)
    totals = jnp.sum(weights, axis=(2, 3), keepdims=True)
    probs = (
        (weights / totals)
        .reshape(query_blocks * block_size, key_blocks * block_size)
        .astype(jnp.bfloat16)
    )
    return jnp.dot(probs, values, preferred_element_type=jnp.float32).astype(jnp.bfloat16)


def shards(section_input, norm_gain, qkv_weight, out_weight, random_blocks, global_blocks):
    token_rows = section_input[0]
    token_count = token_rows.shape[0]
    width = norm_gain.shape[1] * lax.axis_size("dp")
    as_float = token_rows.astype(jnp.float32)
    local_squares = jnp.sum(as_float * as_float, axis=1)
    total_squares = lax.psum(local_squares, "dp")
    factor = lax.rsqrt(total_squares / width + 1e-05)[:, None]
    normed_part = (as_float * factor * norm_gain[0].astype(jnp.float32)).astype(jnp.bfloat16)
    normed = lax.all_gather(normed_part, "dp", axis=1, tiled=True)
    weight_half = qkv_weight[0]
    joined = jnp.dot(
        normed,
        lax.all_gather(weight_half, "seq", axis=0, tiled=True),
        preferred_element_type=jnp.float32,
    )
    head_size = joined.shape[1] // 3
    query = joined[:, :head_size].astype(jnp.bfloat16)
    keys_values = joined[:, head_size:].astype(jnp.bfloat16)
    document_kv = lax.all_gather(keys_values, "seq", axis=0, tiled=True)
    keys = document_kv[:, :head_size]
    values = document_kv[:, head_size:]
    own_blocks = token_count // BLOCK
    query_ids = lax.axis_index("seq") * own_blocks + jnp.arange(own_blocks, dtype=jnp.int32)
    allowed = block_mask(
        query_ids, random_blocks[0], global_blocks[0], document_kv.shape[0] // BLOCK
    )
    attended = sparse_attention(query, keys, values, allowed, BLOCK)
    out_columns = out_weight[0]
    added = jnp.dot(
        lax.all_gather(attended, "dp", axis=1, tiled=True),
        out_columns,
        preferred_element_type=jnp.float32,
    )
    result = (token_rows.astype(jnp.float32) + added).astype(jnp.bfloat16)
    return shifted(result[None], "section", 1)


CHUNKS = 4


def relay_kernel(
    nz,
    x_ref,
    gain_ref,
    w_ref,
    ow_ref,
    rand_ref,
    glob_ref,
    out_ref,
    x_all,
    w_all,
    g_all,
    acc,
    q_s,
    kv,
    bias,
    m_s,
    l_s,
    o_s,
    att_own,
    att_all,
    x_next,
    ow_next,
    w_far,
    part_out,
    part_in,
    ss_out,
    ss_in,
    total_s,
    rand_s,
    xs,
    xr,
    ws,
    wr,
    gs,
    gr,
    ks,
    kr,
    ts,
    tr,
    as_,
    ar,
    ns,
    nr,
    fs,
    fr,
    ps,
    pr,
    local,
):
    sec, p, y = lax.axis_index("section"), lax.axis_index("dp"), lax.axis_index("seq")
    dp = 2 * nz
    z, core = p // 2, p % 2
    sib = p + 1 - 2 * core
    tokens, feats = x_ref.shape
    width = feats * dp
    rows = tokens // CHUNKS
    head = q_s.shape[1]
    half = dp // 2
    scale = math.log2(math.e) / math.sqrt(head)

    barrier = pltpu.get_barrier_semaphore()
    for step in range(1, dp):
        pl.semaphore_signal(
            barrier, inc=1, device_id={"dp": lax.rem(p + step, dp)},
            device_id_type=pl.DeviceIdType.MESH,
        )
    for name, at in (("seq", 1 - y), ("section", 1 - sec)):
        pl.semaphore_signal(
            barrier, inc=1, device_id={name: at}, device_id_type=pl.DeviceIdType.MESH
        )

    def remote(src, dst, send, recv, where):
        return pltpu.make_async_remote_copy(
            src_ref=src, dst_ref=dst, send_sem=send, recv_sem=recv,
            device_id=where, device_id_type=pl.DeviceIdType.MESH,
        )

    def part(k):
        return pl.ds(k * rows, rows)

    def chunk(k):
        return pl.ds(pl.multiple_of(k * rows, rows), rows)

    own_x = pltpu.make_async_copy(x_ref, x_all.at[p], local.at[0])
    own_w = pltpu.make_async_copy(
        w_ref, w_all.at[pl.ds(pl.multiple_of(y * half * feats, feats), half * feats), :], local.at[1]
    )
    rand_copy = pltpu.make_async_copy(rand_ref, rand_s, local.at[2])
    rand_copy.start()
    own_x.start()
    own_w.start()
    g_all[p] = jnp.broadcast_to(gain_ref[...].astype(jnp.float32), (8, feats))

    pl.semaphore_wait(barrier, dp + 1)

    def hop(buf, send, recv, way, b, k, src=None):
        at = buf.at[b, part(k), :]
        to = (p - 2, p + 2, sib)[way]
        return remote(at if src is None else src, at, send.at[way, b, k], recv.at[b, k], {"dp": to})

    def spread(buf, send, recv, b, k, ways, act, src=None):
        if 0 in ways:
            @pl.when(z > 0)
            def _():
                act(hop(buf, send, recv, 0, b, k, src))
        if 1 in ways:
            @pl.when(z < nz - 1)
            def _():
                act(hop(buf, send, recv, 1, b, k, src))
        act(hop(buf, send, recv, 2, b, k, src))

    start = lambda copy: copy.start()
    sent = lambda copy: copy.wait_send()

    def chain(buf, send, recv, d, k):
        @pl.when(z + d < nz)
        def _():
            b = p + 2 * d
            hop(buf, send, recv, 2, b, k).wait_recv()
            spread(buf, send, recv, b, k, (0,), start)

        @pl.when(z - d >= 0)
        def _():
            b = p - 2 * d
            hop(buf, send, recv, 2, b, k).wait_recv()
            spread(buf, send, recv, b, k, (1,), start)

    def drain(buf, send, recv, k, src=None):
        spread(buf, send, recv, p, k, (0, 1), sent, src)
        for d in range(1, nz):
            @pl.when(z + d < nz)
            def _():
                spread(buf, send, recv, p + 2 * d, k, (0,), sent)

            @pl.when(z - d >= 0)
            def _():
                spread(buf, send, recv, p - 2 * d, k, (1,), sent)

    near = z // (nz // 2)
    far = 1 - near
    inward = 2 - 4 * near
    is_end = (z == 0) | (z == nz - 1)
    is_helper = jnp.logical_not(is_end)
    in_far, in_near = y == far, y != far
    mate, end, far_end = p + inward, p - inward, p + 2 * inward

    def other(b):
        return b + 1 - 2 * core

    def xhop(way, b, k, own=False):
        at = x_all.at[b, part(k), :]
        to = (p + inward, p - inward, sib)[way]
        src = x_ref.at[part(k), :] if own else at
        return remote(src, at, xs.at[way, b, k], xr.at[b, k], {"dp": to})

    def arrived(b, k, *ways):
        xhop(2, b, k).wait_recv()
        for way in ways:
            xhop(way, b, k).start()

    def rows_of(j):
        return pl.ds(pl.multiple_of(j * feats, feats), feats)

    def w_copy(j):
        return remote(
            w_ref.at[rows_of(j), :], w_all.at[rows_of(y * half + j), :], ws.at[j], wr.at[j],
            {"seq": 1 - y},
        )

    def far_copy(j, src, where):
        return remote(src, w_far.at[rows_of(j), :], fs.at[j], fr.at[j], where)

    def far_from_end(j):
        return far_copy(j, w_ref.at[rows_of(j), :], {"dp": mate})

    def far_passed(j):
        return far_copy(j, w_all.at[rows_of(far * half + j), :], {"dp": mate})

    def far_shared(j):
        return far_copy(j, w_far.at[rows_of(j), :], {"seq": 1 - y})

    def gain_copy(to, src):
        return remote(g_all.at[src], g_all.at[src], gs.at[to], gr.at[src], {"dp": to})

    quarter = half // 2
    first_w = (1 - y) * quarter
    rest_w = y * quarter

    @pl.when(is_helper)
    def _():
        for k in range(CHUNKS):
            for way in (0, 1, 2):
                xhop(way, p, k, True).start()
        for j in range(quarter):
            w_copy(first_w + j).start()

    @pl.when(is_end & in_far)
    def _():
        far_from_end(0).start()
        w_copy(quarter).start()
        for k in range(CHUNKS):
            xhop(2, p, k, True).start()

    @pl.when(is_end & in_near)
    def _():
        xhop(0, p, 0, True).start()
        for k in range(CHUNKS):
            xhop(2, p, k, True).start()
        for j in range(half):
            w_copy(j).start()

    for step in range(1, dp):
        gain_copy(lax.rem(p + step, dp), p).start()

    next_x = remote(x_ref, x_next, ns.at[0], nr.at[0], {"section": 1 - sec})
    next_w = remote(ow_ref, ow_next, ns.at[1], nr.at[1], {"section": 1 - sec})
    next_x.start()
    next_w.start()

    acc[...] = jnp.zeros_like(acc)

    rand_copy.wait()

    blocks = tokens // BLOCK
    for h in range(2):
        key_at = y if h == 0 else 1 - y
        lane = lax.broadcasted_iota(jnp.int32, (blocks, tokens), 1)
        key_id = lane // BLOCK + key_at * blocks
        query_id = lax.broadcasted_iota(jnp.int32, (blocks, tokens), 0) + y * blocks
        allowed = jnp.abs(query_id - key_id) <= 1
        for g in range(glob_ref.shape[1]):
            number = glob_ref[:, g : g + 1]
            allowed = allowed | (key_id == number) | (query_id == number)
        for r in range(rand_ref.shape[2]):
            allowed = allowed | (key_id == rand_s[0, :, r : r + 1])
        bias[h] = jnp.where(allowed, 0.0, -jnp.inf)

    def scaled(b, k):
        return (x_all[b, chunk(k), :].astype(jnp.float32) * g_all[b, 0:1, :]).astype(jnp.bfloat16)

    def project(b, k):
        acc[chunk(k), :] += jnp.dot(
            scaled(b, k), w_all[rows_of(b), :], preferred_element_type=jnp.float32
        )

    def project_whole(b):
        def body(i, _):
            at = pl.ds(pl.multiple_of(i * 2 * rows, 2 * rows), 2 * rows)
            xg = (x_all[b, at, :].astype(jnp.float32) * g_all[b, 0:1, :]).astype(jnp.bfloat16)
            acc[at, :] += jnp.dot(xg, w_all[rows_of(b), :], preferred_element_type=jnp.float32)
            return 0

        lax.fori_loop(0, CHUNKS // 2, body, 0)

    def from_sib(b, k):
        xhop(2, b, k).wait_recv()

    def kv_copy(k):
        return remote(kv.at[0, part(k), :], kv.at[1, part(k), :], ks.at[k], kr.at[k], {"seq": 1 - y})

    def finish_joined(k, joined, total):
        joined = joined * lax.rsqrt(total / width + 1e-05)
        q_s[part(k), :] = joined[:, :head].astype(jnp.bfloat16)
        kv[0, part(k), :] = joined[:, head:].astype(jnp.bfloat16)
        kv_copy(k).start()

    def part_copies(k):
        return (
            remote(part_out.at[part(k), :], part_in.at[part(k), :], ps.at[0, k], pr.at[0, k], {"dp": end}),
            remote(ss_out.at[k], ss_in.at[k], ps.at[1, k], pr.at[1, k], {"dp": end}),
        )

    def diagonal():
        return lax.broadcasted_iota(jnp.int32, (rows, rows), 0) == lax.broadcasted_iota(
            jnp.int32, (rows, rows), 1
        )

    def help_end(k):
        if k == 0:
            @pl.when(in_far)
            def _():
                for j in range(quarter, half):
                    far_shared(j).wait_recv()

            @pl.when(in_near)
            def _():
                for j in range(quarter):
                    far_shared(j).wait_recv()

        from_sib(other(end), k)
        from_sib(other(far_end), k)
        part_sum = jnp.zeros((rows, acc.shape[1]), jnp.float32)
        for j in range(half):
            part_sum += jnp.dot(
                scaled(far * half + j, k), w_far[pl.ds(j * feats, feats), :],
                preferred_element_type=jnp.float32,
            )
        part_out[part(k), :] = part_sum.astype(jnp.bfloat16)
        folded = jnp.zeros((rows, 128), jnp.float32)
        for b in range(dp):
            for c in range(feats // 128):
                xb = x_all[b, part(k), c * 128 : (c + 1) * 128].astype(jnp.float32)
                folded += xb * xb
        total = jnp.sum(folded, axis=1, keepdims=True)
        total_s[part(k), :] = total
        across = jnp.sum(
            jnp.where(diagonal(), jnp.broadcast_to(total, (rows, rows)), 0.0), axis=0, keepdims=True
        )
        ss_out[k] = jnp.broadcast_to(across, (8, rows))
        for copy in part_copies(k):
            copy.start()

    def all_gains():
        for step in range(1, dp):
            gain_copy(sib, lax.rem(p + step, dp)).wait_recv()

    @pl.when(is_end)
    def _():
        @pl.when(in_far)
        def _():
            for j in range(1, quarter):
                far_from_end(j - 1).wait_send()
                far_from_end(j).start()
                w_copy(quarter + j - 1).wait_send()
                w_copy(quarter + j).start()
            far_from_end(quarter - 1).wait_send()
            xhop(0, p, 0, True).start()

        @pl.when(in_near)
        def _():
            w_copy(quarter).wait_recv()
            xhop(0, p, 0, True).wait_send()
            far_passed(quarter).start()
            for j in range(quarter + 1, half):
                w_copy(j).wait_recv()
                far_passed(j - 1).wait_send()
                far_passed(j).start()

        for k in range(CHUNKS):
            arrived(mate, k, 2)

        @pl.when(in_far)
        def _():
            xhop(0, p, 0, True).wait_send()

        @pl.when(in_near)
        def _():
            far_passed(half - 1).wait_send()

        for k in range(1, CHUNKS):
            xhop(0, p, k, True).start()
            if k < CHUNKS - 1:
                xhop(0, p, k, True).wait_send()
        own_x.wait()
        own_w.wait()
        all_gains()

        @pl.when(in_far)
        def _():
            for j in range(half):
                w_copy(j).wait_recv()

        for k in range(CHUNKS):
            from_sib(sib, k)
            from_sib(other(mate), k)
        for b in (p, sib, mate, other(mate)):
            project_whole(b)
        for k in range(CHUNKS):
            for copy in part_copies(k):
                copy.wait_recv()
            total = jnp.sum(
                jnp.where(diagonal(), jnp.broadcast_to(ss_in[k, 0:1, :], (rows, rows)), 0.0),
                axis=1, keepdims=True,
            )
            finish_joined(k, acc[part(k), :] + part_in[part(k), :].astype(jnp.float32), total)

    @pl.when(is_helper)
    def _():
        def share(j):
            far_shared(j).wait_recv()
            far_shared(j).start()

        def when_far(fn):
            pl.when(in_far)(fn)

        def when_near(fn):
            pl.when(in_near)(fn)

        when_near(lambda: arrived(end, 0, 0, 2))
        when_far(lambda: share(0))
        when_far(lambda: share(1))
        when_near(lambda: share(2))
        for k in range(CHUNKS):
            arrived(mate, k, 2)
        when_far(lambda: arrived(end, 0, 0, 2))
        when_near(lambda: share(3))

        own_x.wait()
        own_w.wait()
        all_gains()
        for j in range(quarter):
            w_copy(rest_w + j).wait_recv()
        for k in range(CHUNKS):
            from_sib(sib, k)
            from_sib(other(mate), k)
        project_whole(p)
        project_whole(sib)
        arrived(end, 1, 0, 2)
        project_whole(mate)
        project_whole(other(mate))
        arrived(end, 2, 0, 2)

        @pl.when(in_far)
        def _():
            for j in range(quarter):
                far_shared(j).wait_send()

        @pl.when(in_near)
        def _():
            for j in range(quarter, half):
                far_shared(j).wait_send()

        for j in range(quarter):
            w_copy(rest_w + j).start()

        held = jnp.where(near == y, end, far_end)
        missing = jnp.where(near == y, far_end, end)

        def help_and_project(k):
            help_end(k)
            project(held, k)
            project(other(held), k)

        for k in range(CHUNKS):
            if k == 2:
                arrived(end, 3, 0, 2)
            arrived(far_end, k, 2)
            if k > 0:
                help_and_project(k - 1)
        help_and_project(CHUNKS - 1)
        for j in range(quarter):
            w_copy(first_w + j).wait_recv()
        for k in range(CHUNKS):
            project(missing, k)
            project(other(missing), k)
            finish_joined(k, acc[part(k), :], total_s[part(k), :])

    per = blocks // CHUNKS

    def scores_of(k, h):
        s = lax.dot_general(
            q_s[part(k), :], kv[h, :, :head], (((1,), (1,)), ((), ())),
            preferred_element_type=jnp.float32,
        )
        s = (s * scale).reshape(per, BLOCK, tokens)
        s = s + bias[h, k * per : (k + 1) * per, :][:, None, :]
        return s.reshape(rows, tokens)

    def own_keys(k):
        s = scores_of(k, 0)
        m = jnp.max(s, axis=1, keepdims=True)
        e = jnp.exp2(s - m)
        m_s[part(k), :] = m
        l_s[part(k), :] = jnp.sum(e, axis=1, keepdims=True)
        o_s[part(k), :] = jnp.dot(
            e.astype(jnp.bfloat16), kv[0, :, head:], preferred_element_type=jnp.float32
        )

    def att_copy(k):
        return remote(
            att_own.at[part(k), :], att_all.at[p, part(k), :], ts.at[k], ar.at[p, k], {"section": 1 - sec}
        )

    def other_keys(k):
        s = scores_of(k, 1)
        before = m_s[part(k), :]
        m = jnp.maximum(before, jnp.max(s, axis=1, keepdims=True))
        e = jnp.exp2(s - m)
        shrink = jnp.exp2(before - m)
        total = l_s[part(k), :] * shrink + jnp.sum(e, axis=1, keepdims=True)
        o = o_s[part(k), :] * shrink + jnp.dot(
            e.astype(jnp.bfloat16), kv[1, :, head:], preferred_element_type=jnp.float32
        )
        att_own[part(k), :] = (o / total).astype(jnp.bfloat16)
        att_copy(k).start()

    for k in range(CHUNKS):
        own_keys(k)
    for k in range(CHUNKS):
        kv_copy(k).wait_recv()
    next_x.wait_recv()
    next_w.wait_recv()

    def att_step(d, k):
        if d == 0:
            att_copy(k).wait_recv()
            spread(att_all, as_, ar, p, k, (0, 1), start)
        else:
            chain(att_all, as_, ar, d, k)

    def finish(k):
        hop(att_all, as_, ar, 2, sib, k).wait_recv()
        for d in range(1, nz):
            @pl.when(z + d < nz)
            def _():
                hop(att_all, as_, ar, 2, sib + 2 * d, k).wait_recv()

            @pl.when(z - d >= 0)
            def _():
                hop(att_all, as_, ar, 2, sib - 2 * d, k).wait_recv()
        heads = jnp.concatenate([att_all[b, part(k), :] for b in range(dp)], axis=1)
        added = jnp.dot(heads, ow_next[...], preferred_element_type=jnp.float32)
        out_ref[part(k), :] = (x_next[part(k), :].astype(jnp.float32) + added).astype(jnp.bfloat16)

    for i in range(CHUNKS + nz + 1):
        if i < CHUNKS:
            other_keys(i)
        for d in range(nz):
            if 0 <= i - 1 - d < CHUNKS:
                att_step(d, i - 1 - d)
        if 0 <= i - nz - 1 < CHUNKS:
            finish(i - nz - 1)

    for k in range(CHUNKS):
        drain(att_all, as_, ar, k)
        kv_copy(k).wait_send()
        att_copy(k).wait_send()
        xhop(2, p, k, True).wait_send()
        xhop(2, mate, k).wait_send()

        @pl.when(is_helper)
        def _():
            xhop(0, p, k, True).wait_send()
            xhop(1, p, k, True).wait_send()
            xhop(0, end, k).wait_send()
            xhop(2, end, k).wait_send()
            xhop(2, far_end, k).wait_send()
            for copy in part_copies(k):
                copy.wait_send()

    for step in range(1, dp):
        gain_copy(lax.rem(p + step, dp), p).wait_send()
    @pl.when(is_end)
    def _():
        xhop(0, p, CHUNKS - 1, True).wait_send()

    @pl.when(is_end & in_far)
    def _():
        w_copy(half - 1).wait_send()

    @pl.when(jnp.logical_not(is_end & in_far))
    def _():
        for j in range(half):
            w_copy(j).wait_send()

    next_x.wait_send()
    next_w.wait_send()


def relay(dp, x, gain, w, ow, rand, glob):
    nz = dp // 2
    tokens, feats = x.shape
    columns = w.shape[1]
    head = columns // 3
    vmem = pl.BlockSpec(memory_space=pltpu.VMEM)
    anywhere = pl.BlockSpec(memory_space=pl.ANY)
    bf16, f32, dma = jnp.bfloat16, jnp.float32, pltpu.SemaphoreType.DMA
    return pl.pallas_call(
        functools.partial(relay_kernel, nz),
        out_shape=jax.ShapeDtypeStruct((tokens, feats), bf16),
        in_specs=[anywhere, vmem, anywhere, anywhere, anywhere, vmem],
        out_specs=vmem,
        scratch_shapes=[
            pltpu.VMEM((dp, tokens, feats), bf16),
            pltpu.VMEM((dp * feats, columns), bf16),
            pltpu.VMEM((dp, 8, feats), f32),
            pltpu.VMEM((tokens, columns), f32),
            pltpu.VMEM((tokens, head), bf16),
            pltpu.VMEM((2, tokens, 2 * head), bf16),
            pltpu.VMEM((2, tokens // BLOCK, tokens), f32),
            pltpu.VMEM((tokens, 1), f32),
            pltpu.VMEM((tokens, 1), f32),
            pltpu.VMEM((tokens, head), f32),
            pltpu.VMEM((tokens, head), bf16),
            pltpu.VMEM((dp, tokens, head), bf16),
            pltpu.VMEM((tokens, feats), bf16),
            pltpu.VMEM(ow.shape, bf16),
            pltpu.VMEM((dp // 2 * feats, columns), bf16),
            pltpu.VMEM((tokens, columns), bf16),
            pltpu.VMEM((tokens, columns), bf16),
            pltpu.VMEM((CHUNKS, 8, tokens // CHUNKS), f32),
            pltpu.VMEM((CHUNKS, 8, tokens // CHUNKS), f32),
            pltpu.VMEM((tokens, 1), f32),
            pltpu.VMEM(rand.shape, jnp.int32),
            dma((3, dp, CHUNKS)),
            dma((dp, CHUNKS)),
            dma((dp // 2,)),
            dma((dp // 2,)),
            dma((dp,)),
            dma((dp,)),
            dma((CHUNKS,)),
            dma((CHUNKS,)),
            dma((CHUNKS,)),
            dma((CHUNKS,)),
            dma((3, dp, CHUNKS)),
            dma((dp, CHUNKS)),
            dma((2,)),
            dma((2,)),
            dma((dp // 2,)),
            dma((dp // 2,)),
            dma((2, CHUNKS)),
            dma((2, CHUNKS)),
            dma((3,)),
        ],
        compiler_params=pltpu.CompilerParams(
            collective_id=0, has_side_effects=True, vmem_limit_bytes=56 * 1024 * 1024
        ),
        name="relay_layer",
    )(x, gain, w, ow, rand, glob)


def tiles(mesh, tokens, feats, columns):
    return (
        mesh.shape["section"] == 2
        and mesh.shape["seq"] == 2
        and mesh.shape["dp"] == 8
        and feats % 128 == 0
        and columns % 384 == 0
        and tokens % (CHUNKS * BLOCK) == 0
    )


def solution(mesh):
    placed = (
        P("section", "seq", "dp"),
        P("section", "dp"),
        P("section", "seq", "dp"),
        P("section", None, "dp"),
        P("section", "seq", None),
        P("section", None),
    )

    def layer(section_input, norm_gain, qkv_weight, out_weight, random_blocks, global_blocks):
        args = (section_input, norm_gain, qkv_weight, out_weight, random_blocks, global_blocks)
        _, tokens, feats = section_input.shape
        if not tiles(mesh, tokens, feats, qkv_weight.shape[2]):
            return shards(*args)
        out = relay(
            mesh.shape["dp"], section_input[0], norm_gain, qkv_weight[0], out_weight[0],
            random_blocks, global_blocks,
        )
        return out[None]

    return jax.shard_map(
        layer, mesh=mesh, in_specs=placed, out_specs=P("section", "seq", "dp"), check_vma=False
    )
```

```python
import functools
import math

import jax
import jax.numpy as jnp
from jax import lax
from jax.experimental import pallas as pl
from jax.experimental.pallas import tpu as pltpu
from jax.sharding import PartitionSpec as P

BLOCK = 64


def shifted(block, axis, distance):
    devices = range(lax.axis_size(axis))
    route = [((i - distance) % len(devices), i) for i in devices]
    return lax.ppermute(block, axis, route)


def block_mask(query_ids, random_rows, global_ids, key_count):
    query_col = query_ids[:, None]
    key_ids = jnp.arange(key_count, dtype=jnp.int32)[None, :]
    adjacent = jnp.abs(query_col - key_ids) <= 1
    key_global = jnp.any(key_ids[:, :, None] == global_ids[None, None, :], axis=2)
    query_global = jnp.any(query_col[:, :, None] == global_ids[None, None, :], axis=2)
    chosen = jnp.any(random_rows[:, None, :] == key_ids[:, :, None], axis=2)
    return adjacent | key_global | query_global | chosen


def sparse_attention(query, keys, values, allowed, block_size):
    scores = lax.dot_general(
        query, keys, (((1,), (1,)), ((), ())), preferred_element_type=jnp.float32
    )
    scores = scores * (1.0 / math.sqrt(query.shape[1]))
    query_blocks, key_blocks = allowed.shape
    scores = scores.reshape(query_blocks, block_size, key_blocks, block_size)
    live = allowed[:, None, :, None]
    scores = jnp.where(live, scores, -1e30)
    highest = jnp.max(scores, axis=(2, 3), keepdims=True)
    weights = jnp.where(live, jnp.exp(scores - highest), 0.0)
    totals = jnp.sum(weights, axis=(2, 3), keepdims=True)
    probs = (
        (weights / totals)
        .reshape(query_blocks * block_size, key_blocks * block_size)
        .astype(jnp.bfloat16)
    )
    return jnp.dot(probs, values, preferred_element_type=jnp.float32).astype(jnp.bfloat16)


def shards(section_input, norm_gain, qkv_weight, out_weight, random_blocks, global_blocks):
    token_rows = section_input[0]
    token_count = token_rows.shape[0]
    width = norm_gain.shape[1] * lax.axis_size("dp")
    as_float = token_rows.astype(jnp.float32)
    local_squares = jnp.sum(as_float * as_float, axis=1)
    total_squares = lax.psum(local_squares, "dp")
    factor = lax.rsqrt(total_squares / width + 1e-05)[:, None]
    normed_part = (as_float * factor * norm_gain[0].astype(jnp.float32)).astype(jnp.bfloat16)
    normed = lax.all_gather(normed_part, "dp", axis=1, tiled=True)
    weight_half = qkv_weight[0]
    joined = jnp.dot(
        normed,
        lax.all_gather(weight_half, "seq", axis=0, tiled=True),
        preferred_element_type=jnp.float32,
    )
    head_size = joined.shape[1] // 3
    query = joined[:, :head_size].astype(jnp.bfloat16)
    keys_values = joined[:, head_size:].astype(jnp.bfloat16)
    document_kv = lax.all_gather(keys_values, "seq", axis=0, tiled=True)
    keys = document_kv[:, :head_size]
    values = document_kv[:, head_size:]
    own_blocks = token_count // BLOCK
    query_ids = lax.axis_index("seq") * own_blocks + jnp.arange(own_blocks, dtype=jnp.int32)
    allowed = block_mask(
        query_ids, random_blocks[0], global_blocks[0], document_kv.shape[0] // BLOCK
    )
    attended = sparse_attention(query, keys, values, allowed, BLOCK)
    out_columns = out_weight[0]
    added = jnp.dot(
        lax.all_gather(attended, "dp", axis=1, tiled=True),
        out_columns,
        preferred_element_type=jnp.float32,
    )
    result = (token_rows.astype(jnp.float32) + added).astype(jnp.bfloat16)
    return shifted(result[None], "section", 1)


CHUNKS = 4
QUERIES = 8


def relay_kernel(
    nz,
    x_ref,
    gain_ref,
    w_ref,
    ow_ref,
    rand_ref,
    glob_ref,
    out_ref,
    x_all,
    w_all,
    g_all,
    acc,
    q_s,
    kv,
    bias,
    m_s,
    l_s,
    o_s,
    att_own,
    att_all,
    x_next,
    ow_next,
    w_far,
    part_out,
    part_in,
    ss_out,
    ss_in,
    total_s,
    rand_s,
    xs,
    xr,
    ws,
    wr,
    gs,
    gr,
    ks,
    kr,
    ts,
    tr,
    as_,
    ar,
    ns,
    nr,
    fs,
    fr,
    ps,
    pr,
    local,
):
    sec, p, y = lax.axis_index("section"), lax.axis_index("dp"), lax.axis_index("seq")
    dp = 2 * nz
    z, core = p // 2, p % 2
    sib = p + 1 - 2 * core
    tokens, feats = x_ref.shape
    width = feats * dp
    rows = tokens // CHUNKS
    head = q_s.shape[1]
    half = dp // 2
    scale = math.log2(math.e) / math.sqrt(head)

    barrier = pltpu.get_barrier_semaphore()
    for step in range(1, dp):
        pl.semaphore_signal(
            barrier, inc=1, device_id={"dp": lax.rem(p + step, dp)},
            device_id_type=pl.DeviceIdType.MESH,
        )
    for name, at in (("seq", 1 - y), ("section", 1 - sec)):
        pl.semaphore_signal(
            barrier, inc=1, device_id={name: at}, device_id_type=pl.DeviceIdType.MESH
        )

    def remote(src, dst, send, recv, where):
        return pltpu.make_async_remote_copy(
            src_ref=src, dst_ref=dst, send_sem=send, recv_sem=recv,
            device_id=where, device_id_type=pl.DeviceIdType.MESH,
        )

    def part(k):
        return pl.ds(k * rows, rows)

    few = tokens // QUERIES

    def apart(k):
        return pl.ds(k * few, few)

    def chunk(k):
        return pl.ds(pl.multiple_of(k * rows, rows), rows)

    own_x = pltpu.make_async_copy(x_ref, x_all.at[p], local.at[0])
    own_w = pltpu.make_async_copy(
        w_ref, w_all.at[pl.ds(pl.multiple_of(y * half * feats, feats), half * feats), :], local.at[1]
    )
    rand_copy = pltpu.make_async_copy(rand_ref, rand_s, local.at[2])
    rand_copy.start()
    own_x.start()
    own_w.start()
    g_all[p] = jnp.broadcast_to(gain_ref[...].astype(jnp.float32), (8, feats))

    pl.semaphore_wait(barrier, dp + 1)

    def hop(buf, send, recv, way, b, k, src=None):
        at = buf.at[b, apart(k), :]
        to = (p - 2, p + 2, sib)[way]
        return remote(at if src is None else src, at, send.at[way, b, k], recv.at[b, k], {"dp": to})

    def spread(buf, send, recv, b, k, ways, act, src=None):
        if 0 in ways:
            @pl.when(z > 0)
            def _():
                act(hop(buf, send, recv, 0, b, k, src))
        if 1 in ways:
            @pl.when(z < nz - 1)
            def _():
                act(hop(buf, send, recv, 1, b, k, src))
        act(hop(buf, send, recv, 2, b, k, src))

    start = lambda copy: copy.start()
    sent = lambda copy: copy.wait_send()

    def chain(buf, send, recv, d, k):
        @pl.when(z + d < nz)
        def _():
            b = p + 2 * d
            hop(buf, send, recv, 2, b, k).wait_recv()
            spread(buf, send, recv, b, k, (0,), start)

        @pl.when(z - d >= 0)
        def _():
            b = p - 2 * d
            hop(buf, send, recv, 2, b, k).wait_recv()
            spread(buf, send, recv, b, k, (1,), start)

    def drain(buf, send, recv, k, src=None):
        spread(buf, send, recv, p, k, (0, 1), sent, src)
        for d in range(1, nz):
            @pl.when(z + d < nz)
            def _():
                spread(buf, send, recv, p + 2 * d, k, (0,), sent)

            @pl.when(z - d >= 0)
            def _():
                spread(buf, send, recv, p - 2 * d, k, (1,), sent)

    near = z // (nz // 2)
    far = 1 - near
    inward = 2 - 4 * near
    is_end = (z == 0) | (z == nz - 1)
    is_helper = jnp.logical_not(is_end)
    in_far, in_near = y == far, y != far
    mate, end, far_end = p + inward, p - inward, p + 2 * inward

    def other(b):
        return b + 1 - 2 * core

    def xhop(way, b, k, own=False):
        at = x_all.at[b, part(k), :]
        to = (p + inward, p - inward, sib)[way]
        src = x_ref.at[part(k), :] if own else at
        return remote(src, at, xs.at[way, b, k], xr.at[b, k], {"dp": to})

    def arrived(b, k, *ways):
        xhop(2, b, k).wait_recv()
        for way in ways:
            xhop(way, b, k).start()

    def rows_of(j):
        return pl.ds(pl.multiple_of(j * feats, feats), feats)

    def w_copy(j):
        return remote(
            w_ref.at[rows_of(j), :], w_all.at[rows_of(y * half + j), :], ws.at[j], wr.at[j],
            {"seq": 1 - y},
        )

    def far_copy(j, src, where):
        return remote(src, w_far.at[rows_of(j), :], fs.at[j], fr.at[j], where)

    def far_from_end(j):
        return far_copy(j, w_ref.at[rows_of(j), :], {"dp": mate})

    def far_passed(j):
        return far_copy(j, w_all.at[rows_of(far * half + j), :], {"dp": mate})

    def far_shared(j):
        return far_copy(j, w_far.at[rows_of(j), :], {"seq": 1 - y})

    def gain_copy(to, src):
        return remote(g_all.at[src], g_all.at[src], gs.at[to], gr.at[src], {"dp": to})

    quarter = half // 2
    first_w = (1 - y) * quarter
    rest_w = y * quarter

    @pl.when(is_helper)
    def _():
        for k in range(CHUNKS):
            for way in (0, 1, 2):
                xhop(way, p, k, True).start()
        for j in range(quarter):
            w_copy(first_w + j).start()

    @pl.when(is_end & in_far)
    def _():
        far_from_end(0).start()
        w_copy(quarter).start()
        for k in range(CHUNKS):
            xhop(2, p, k, True).start()

    @pl.when(is_end & in_near)
    def _():
        xhop(0, p, 0, True).start()
        for k in range(CHUNKS):
            xhop(2, p, k, True).start()
        for j in range(half):
            w_copy(j).start()

    for step in range(1, dp):
        gain_copy(lax.rem(p + step, dp), p).start()

    next_x = remote(x_ref, x_next, ns.at[0], nr.at[0], {"section": 1 - sec})
    next_w = remote(ow_ref, ow_next, ns.at[1], nr.at[1], {"section": 1 - sec})
    next_x.start()
    next_w.start()

    acc[...] = jnp.zeros_like(acc)

    rand_copy.wait()

    blocks = tokens // BLOCK
    for h in range(2):
        key_at = y if h == 0 else 1 - y
        lane = lax.broadcasted_iota(jnp.int32, (blocks, tokens), 1)
        key_id = lane // BLOCK + key_at * blocks
        query_id = lax.broadcasted_iota(jnp.int32, (blocks, tokens), 0) + y * blocks
        allowed = jnp.abs(query_id - key_id) <= 1
        for g in range(glob_ref.shape[1]):
            number = glob_ref[:, g : g + 1]
            allowed = allowed | (key_id == number) | (query_id == number)
        for r in range(rand_ref.shape[2]):
            allowed = allowed | (key_id == rand_s[0, :, r : r + 1])
        bias[h] = jnp.where(allowed, 0.0, -jnp.inf)

    def scaled(b, k):
        return (x_all[b, chunk(k), :].astype(jnp.float32) * g_all[b, 0:1, :]).astype(jnp.bfloat16)

    def project(b, k):
        acc[chunk(k), :] += jnp.dot(
            scaled(b, k), w_all[rows_of(b), :], preferred_element_type=jnp.float32
        )

    def project_whole(b):
        def body(i, _):
            at = pl.ds(pl.multiple_of(i * 2 * rows, 2 * rows), 2 * rows)
            xg = (x_all[b, at, :].astype(jnp.float32) * g_all[b, 0:1, :]).astype(jnp.bfloat16)
            acc[at, :] += jnp.dot(xg, w_all[rows_of(b), :], preferred_element_type=jnp.float32)
            return 0

        lax.fori_loop(0, CHUNKS // 2, body, 0)

    def from_sib(b, k):
        xhop(2, b, k).wait_recv()

    def kv_copy(k):
        return remote(kv.at[0, part(k), :], kv.at[1, part(k), :], ks.at[k], kr.at[k], {"seq": 1 - y})

    def finish_joined(k, joined, total):
        joined = joined * lax.rsqrt(total / width + 1e-05)
        q_s[part(k), :] = joined[:, :head].astype(jnp.bfloat16)
        kv[0, part(k), :] = joined[:, head:].astype(jnp.bfloat16)
        kv_copy(k).start()

    def part_copies(k):
        return (
            remote(part_out.at[part(k), :], part_in.at[part(k), :], ps.at[0, k], pr.at[0, k], {"dp": end}),
            remote(ss_out.at[k], ss_in.at[k], ps.at[1, k], pr.at[1, k], {"dp": end}),
        )

    def diagonal():
        return lax.broadcasted_iota(jnp.int32, (rows, rows), 0) == lax.broadcasted_iota(
            jnp.int32, (rows, rows), 1
        )

    def help_end(k):
        if k == 0:
            @pl.when(in_far)
            def _():
                for j in range(quarter, half):
                    far_shared(j).wait_recv()

            @pl.when(in_near)
            def _():
                for j in range(quarter):
                    far_shared(j).wait_recv()

        from_sib(other(end), k)
        from_sib(other(far_end), k)
        part_sum = jnp.zeros((rows, acc.shape[1]), jnp.float32)
        for j in range(half):
            part_sum += jnp.dot(
                scaled(far * half + j, k), w_far[pl.ds(j * feats, feats), :],
                preferred_element_type=jnp.float32,
            )
        part_out[part(k), :] = part_sum.astype(jnp.bfloat16)
        folded = jnp.zeros((rows, 128), jnp.float32)
        for b in range(dp):
            for c in range(feats // 128):
                xb = x_all[b, part(k), c * 128 : (c + 1) * 128].astype(jnp.float32)
                folded += xb * xb
        total = jnp.sum(folded, axis=1, keepdims=True)
        total_s[part(k), :] = total
        across = jnp.sum(
            jnp.where(diagonal(), jnp.broadcast_to(total, (rows, rows)), 0.0), axis=0, keepdims=True
        )
        ss_out[k] = jnp.broadcast_to(across, (8, rows))
        for copy in part_copies(k):
            copy.start()

    def all_gains():
        for step in range(1, dp):
            gain_copy(sib, lax.rem(p + step, dp)).wait_recv()

    @pl.when(is_end)
    def _():
        @pl.when(in_far)
        def _():
            for j in range(1, quarter):
                far_from_end(j - 1).wait_send()
                far_from_end(j).start()
                w_copy(quarter + j - 1).wait_send()
                w_copy(quarter + j).start()
            far_from_end(quarter - 1).wait_send()
            xhop(0, p, 0, True).start()

        @pl.when(in_near)
        def _():
            w_copy(quarter).wait_recv()
            xhop(0, p, 0, True).wait_send()
            far_passed(quarter).start()
            for j in range(quarter + 1, half):
                w_copy(j).wait_recv()
                far_passed(j - 1).wait_send()
                far_passed(j).start()

        for k in range(CHUNKS):
            arrived(mate, k, 2)

        @pl.when(in_far)
        def _():
            xhop(0, p, 0, True).wait_send()

        @pl.when(in_near)
        def _():
            far_passed(half - 1).wait_send()

        for k in range(1, CHUNKS):
            xhop(0, p, k, True).start()
            if k < CHUNKS - 1:
                xhop(0, p, k, True).wait_send()
        own_x.wait()
        own_w.wait()
        all_gains()

        @pl.when(in_far)
        def _():
            for j in range(half):
                w_copy(j).wait_recv()

        for k in range(CHUNKS):
            from_sib(sib, k)
            from_sib(other(mate), k)
        for b in (p, sib, mate, other(mate)):
            project_whole(b)
        for k in range(CHUNKS):
            for copy in part_copies(k):
                copy.wait_recv()
            total = jnp.sum(
                jnp.where(diagonal(), jnp.broadcast_to(ss_in[k, 0:1, :], (rows, rows)), 0.0),
                axis=1, keepdims=True,
            )
            finish_joined(k, acc[part(k), :] + part_in[part(k), :].astype(jnp.float32), total)

    @pl.when(is_helper)
    def _():
        def share(j):
            far_shared(j).wait_recv()
            far_shared(j).start()

        def when_far(fn):
            pl.when(in_far)(fn)

        def when_near(fn):
            pl.when(in_near)(fn)

        when_near(lambda: arrived(end, 0, 0, 2))
        when_far(lambda: share(0))
        when_far(lambda: share(1))
        when_near(lambda: share(2))
        for k in range(CHUNKS):
            arrived(mate, k, 2)
        when_far(lambda: arrived(end, 0, 0, 2))
        when_near(lambda: share(3))

        own_x.wait()
        own_w.wait()
        all_gains()
        for j in range(quarter):
            w_copy(rest_w + j).wait_recv()
        for k in range(CHUNKS):
            from_sib(sib, k)
            from_sib(other(mate), k)
        project_whole(p)
        project_whole(sib)
        arrived(end, 1, 0, 2)
        project_whole(mate)
        project_whole(other(mate))
        arrived(end, 2, 0, 2)

        @pl.when(in_far)
        def _():
            for j in range(quarter):
                far_shared(j).wait_send()

        @pl.when(in_near)
        def _():
            for j in range(quarter, half):
                far_shared(j).wait_send()

        for j in range(quarter):
            w_copy(rest_w + j).start()

        held = jnp.where(near == y, end, far_end)
        missing = jnp.where(near == y, far_end, end)

        def help_and_project(k):
            help_end(k)
            project(held, k)
            project(other(held), k)

        for k in range(CHUNKS):
            if k == 2:
                arrived(end, 3, 0, 2)
            arrived(far_end, k, 2)
            if k > 0:
                help_and_project(k - 1)
        help_and_project(CHUNKS - 1)
        for j in range(quarter):
            w_copy(first_w + j).wait_recv()
        for k in range(CHUNKS):
            project(missing, k)
            project(other(missing), k)
            finish_joined(k, acc[part(k), :], total_s[part(k), :])

    per = blocks // QUERIES

    def scores_of(k, h):
        s = lax.dot_general(
            q_s[apart(k), :], kv[h, :, :head], (((1,), (1,)), ((), ())),
            preferred_element_type=jnp.float32,
        )
        s = (s * scale).reshape(per, BLOCK, tokens)
        s = s + bias[h, k * per : (k + 1) * per, :][:, None, :]
        return s.reshape(few, tokens)

    def own_keys(k):
        s = scores_of(k, 0)
        m = jnp.max(s, axis=1, keepdims=True)
        e = jnp.exp2(s - m)
        m_s[apart(k), :] = m
        l_s[apart(k), :] = jnp.sum(e, axis=1, keepdims=True)
        o_s[apart(k), :] = jnp.dot(
            e.astype(jnp.bfloat16), kv[0, :, head:], preferred_element_type=jnp.float32
        )

    def att_copy(k):
        return remote(
            att_own.at[apart(k), :], att_all.at[p, apart(k), :], ts.at[k], ar.at[p, k], {"section": 1 - sec}
        )

    def other_keys(k):
        s = scores_of(k, 1)
        before = m_s[apart(k), :]
        m = jnp.maximum(before, jnp.max(s, axis=1, keepdims=True))
        e = jnp.exp2(s - m)
        shrink = jnp.exp2(before - m)
        total = l_s[apart(k), :] * shrink + jnp.sum(e, axis=1, keepdims=True)
        o = o_s[apart(k), :] * shrink + jnp.dot(
            e.astype(jnp.bfloat16), kv[1, :, head:], preferred_element_type=jnp.float32
        )
        att_own[apart(k), :] = (o / total).astype(jnp.bfloat16)
        att_copy(k).start()

    for k in range(2):
        own_keys(k)
    for k in range(CHUNKS):
        kv_copy(k).wait_recv()

    def att_step(d, k):
        if d == 0:
            att_copy(k).wait_recv()
            spread(att_all, as_, ar, p, k, (0, 1), start)
        else:
            chain(att_all, as_, ar, d, k)

    def gathered(k):
        hop(att_all, as_, ar, 2, sib, k).wait_recv()
        for d in range(1, nz):
            @pl.when(z + d < nz)
            def _():
                hop(att_all, as_, ar, 2, sib + 2 * d, k).wait_recv()

            @pl.when(z - d >= 0)
            def _():
                hop(att_all, as_, ar, 2, sib - 2 * d, k).wait_recv()

    def finish(k):
        at = part(k)
        heads = jnp.concatenate([att_all[b, at, :] for b in range(dp)], axis=1)
        added = jnp.dot(heads, ow_next[...], preferred_element_type=jnp.float32)
        out_ref[at, :] = (x_next[at, :].astype(jnp.float32) + added).astype(jnp.bfloat16)

    split = QUERIES // CHUNKS
    for i in range(QUERIES + nz + 1):
        if i < QUERIES:
            other_keys(i)
            if i + 2 < QUERIES:
                own_keys(i + 2)
        for d in range(nz):
            if 0 <= i - 1 - d < QUERIES:
                att_step(d, i - 1 - d)
        done = i - nz - 1
        if done == 0:
            next_x.wait_recv()
            next_w.wait_recv()
        if 0 <= done < QUERIES:
            gathered(done)
            if done % split == split - 1:
                finish(done // split)

    for k in range(QUERIES):
        drain(att_all, as_, ar, k)
        att_copy(k).wait_send()
    for k in range(CHUNKS):
        kv_copy(k).wait_send()
        xhop(2, p, k, True).wait_send()
        xhop(2, mate, k).wait_send()

        @pl.when(is_helper)
        def _():
            xhop(0, p, k, True).wait_send()
            xhop(1, p, k, True).wait_send()
            xhop(0, end, k).wait_send()
            xhop(2, end, k).wait_send()
            xhop(2, far_end, k).wait_send()
            for copy in part_copies(k):
                copy.wait_send()

    for step in range(1, dp):
        gain_copy(lax.rem(p + step, dp), p).wait_send()
    @pl.when(is_end)
    def _():
        xhop(0, p, CHUNKS - 1, True).wait_send()

    @pl.when(is_end & in_far)
    def _():
        w_copy(half - 1).wait_send()

    @pl.when(jnp.logical_not(is_end & in_far))
    def _():
        for j in range(half):
            w_copy(j).wait_send()

    next_x.wait_send()
    next_w.wait_send()


def relay(dp, x, gain, w, ow, rand, glob):
    nz = dp // 2
    tokens, feats = x.shape
    columns = w.shape[1]
    head = columns // 3
    vmem = pl.BlockSpec(memory_space=pltpu.VMEM)
    anywhere = pl.BlockSpec(memory_space=pl.ANY)
    bf16, f32, dma = jnp.bfloat16, jnp.float32, pltpu.SemaphoreType.DMA
    return pl.pallas_call(
        functools.partial(relay_kernel, nz),
        out_shape=jax.ShapeDtypeStruct((tokens, feats), bf16),
        in_specs=[anywhere, vmem, anywhere, anywhere, anywhere, vmem],
        out_specs=vmem,
        scratch_shapes=[
            pltpu.VMEM((dp, tokens, feats), bf16),
            pltpu.VMEM((dp * feats, columns), bf16),
            pltpu.VMEM((dp, 8, feats), f32),
            pltpu.VMEM((tokens, columns), f32),
            pltpu.VMEM((tokens, head), bf16),
            pltpu.VMEM((2, tokens, 2 * head), bf16),
            pltpu.VMEM((2, tokens // BLOCK, tokens), f32),
            pltpu.VMEM((tokens, 1), f32),
            pltpu.VMEM((tokens, 1), f32),
            pltpu.VMEM((tokens, head), f32),
            pltpu.VMEM((tokens, head), bf16),
            pltpu.VMEM((dp, tokens, head), bf16),
            pltpu.VMEM((tokens, feats), bf16),
            pltpu.VMEM(ow.shape, bf16),
            pltpu.VMEM((dp // 2 * feats, columns), bf16),
            pltpu.VMEM((tokens, columns), bf16),
            pltpu.VMEM((tokens, columns), bf16),
            pltpu.VMEM((CHUNKS, 8, tokens // CHUNKS), f32),
            pltpu.VMEM((CHUNKS, 8, tokens // CHUNKS), f32),
            pltpu.VMEM((tokens, 1), f32),
            pltpu.VMEM(rand.shape, jnp.int32),
            dma((3, dp, CHUNKS)),
            dma((dp, CHUNKS)),
            dma((dp // 2,)),
            dma((dp // 2,)),
            dma((dp,)),
            dma((dp,)),
            dma((CHUNKS,)),
            dma((CHUNKS,)),
            dma((QUERIES,)),
            dma((QUERIES,)),
            dma((3, dp, QUERIES)),
            dma((dp, QUERIES)),
            dma((2,)),
            dma((2,)),
            dma((dp // 2,)),
            dma((dp // 2,)),
            dma((2, CHUNKS)),
            dma((2, CHUNKS)),
            dma((3,)),
        ],
        compiler_params=pltpu.CompilerParams(
            collective_id=0, has_side_effects=True, vmem_limit_bytes=56 * 1024 * 1024
        ),
        name="relay_layer",
    )(x, gain, w, ow, rand, glob)


def tiles(mesh, tokens, feats, columns):
    return (
        mesh.shape["section"] == 2
        and mesh.shape["seq"] == 2
        and mesh.shape["dp"] == 8
        and feats % 128 == 0
        and columns % 384 == 0
        and tokens % (QUERIES * BLOCK) == 0
    )


def solution(mesh):
    placed = (
        P("section", "seq", "dp"),
        P("section", "dp"),
        P("section", "seq", "dp"),
        P("section", None, "dp"),
        P("section", "seq", None),
        P("section", None),
    )

    def layer(section_input, norm_gain, qkv_weight, out_weight, random_blocks, global_blocks):
        args = (section_input, norm_gain, qkv_weight, out_weight, random_blocks, global_blocks)
        _, tokens, feats = section_input.shape
        if not tiles(mesh, tokens, feats, qkv_weight.shape[2]):
            return shards(*args)
        out = relay(
            mesh.shape["dp"], section_input[0], norm_gain, qkv_weight[0], out_weight[0],
            random_blocks, global_blocks,
        )
        return out[None]

    return jax.shard_map(
        layer, mesh=mesh, in_specs=placed, out_specs=P("section", "seq", "dp"), check_vma=False
    )
```

```python
import functools
import math

import jax
import jax.numpy as jnp
from jax import lax
from jax.experimental import pallas as pl
from jax.experimental.pallas import tpu as pltpu
from jax.sharding import PartitionSpec as P

BLOCK = 64


def shifted(block, axis, distance):
    devices = range(lax.axis_size(axis))
    route = [((i - distance) % len(devices), i) for i in devices]
    return lax.ppermute(block, axis, route)


def block_mask(query_ids, random_rows, global_ids, key_count):
    query_col = query_ids[:, None]
    key_ids = jnp.arange(key_count, dtype=jnp.int32)[None, :]
    adjacent = jnp.abs(query_col - key_ids) <= 1
    key_global = jnp.any(key_ids[:, :, None] == global_ids[None, None, :], axis=2)
    query_global = jnp.any(query_col[:, :, None] == global_ids[None, None, :], axis=2)
    chosen = jnp.any(random_rows[:, None, :] == key_ids[:, :, None], axis=2)
    return adjacent | key_global | query_global | chosen


def sparse_attention(query, keys, values, allowed, block_size):
    scores = lax.dot_general(
        query, keys, (((1,), (1,)), ((), ())), preferred_element_type=jnp.float32
    )
    scores = scores * (1.0 / math.sqrt(query.shape[1]))
    query_blocks, key_blocks = allowed.shape
    scores = scores.reshape(query_blocks, block_size, key_blocks, block_size)
    live = allowed[:, None, :, None]
    scores = jnp.where(live, scores, -1e30)
    highest = jnp.max(scores, axis=(2, 3), keepdims=True)
    weights = jnp.where(live, jnp.exp(scores - highest), 0.0)
    totals = jnp.sum(weights, axis=(2, 3), keepdims=True)
    probs = (
        (weights / totals)
        .reshape(query_blocks * block_size, key_blocks * block_size)
        .astype(jnp.bfloat16)
    )
    return jnp.dot(probs, values, preferred_element_type=jnp.float32).astype(jnp.bfloat16)


def shards(section_input, norm_gain, qkv_weight, out_weight, random_blocks, global_blocks):
    token_rows = section_input[0]
    token_count = token_rows.shape[0]
    width = norm_gain.shape[1] * lax.axis_size("dp")
    as_float = token_rows.astype(jnp.float32)
    local_squares = jnp.sum(as_float * as_float, axis=1)
    total_squares = lax.psum(local_squares, "dp")
    factor = lax.rsqrt(total_squares / width + 1e-05)[:, None]
    normed_part = (as_float * factor * norm_gain[0].astype(jnp.float32)).astype(jnp.bfloat16)
    normed = lax.all_gather(normed_part, "dp", axis=1, tiled=True)
    weight_half = qkv_weight[0]
    joined = jnp.dot(
        normed,
        lax.all_gather(weight_half, "seq", axis=0, tiled=True),
        preferred_element_type=jnp.float32,
    )
    head_size = joined.shape[1] // 3
    query = joined[:, :head_size].astype(jnp.bfloat16)
    keys_values = joined[:, head_size:].astype(jnp.bfloat16)
    document_kv = lax.all_gather(keys_values, "seq", axis=0, tiled=True)
    keys = document_kv[:, :head_size]
    values = document_kv[:, head_size:]
    own_blocks = token_count // BLOCK
    query_ids = lax.axis_index("seq") * own_blocks + jnp.arange(own_blocks, dtype=jnp.int32)
    allowed = block_mask(
        query_ids, random_blocks[0], global_blocks[0], document_kv.shape[0] // BLOCK
    )
    attended = sparse_attention(query, keys, values, allowed, BLOCK)
    out_columns = out_weight[0]
    added = jnp.dot(
        lax.all_gather(attended, "dp", axis=1, tiled=True),
        out_columns,
        preferred_element_type=jnp.float32,
    )
    result = (token_rows.astype(jnp.float32) + added).astype(jnp.bfloat16)
    return shifted(result[None], "section", 1)


CHUNKS = 4


def relay_kernel(
    nz,
    x_ref,
    gain_ref,
    w_ref,
    ow_ref,
    rand_ref,
    glob_ref,
    out_ref,
    x_all,
    w_all,
    g_all,
    acc,
    q_s,
    kv,
    bias,
    m_s,
    l_s,
    o_s,
    att_own,
    att_all,
    x_next,
    ow_next,
    w_far,
    part_out,
    part_in,
    ss_out,
    ss_in,
    total_s,
    rand_s,
    xs,
    xr,
    ws,
    wr,
    gs,
    gr,
    ks,
    kr,
    ts,
    tr,
    as_,
    ar,
    ns,
    nr,
    fs,
    fr,
    ps,
    pr,
    local,
):
    sec, p, y = lax.axis_index("section"), lax.axis_index("dp"), lax.axis_index("seq")
    dp = 2 * nz
    z, core = p // 2, p % 2
    sib = p + 1 - 2 * core
    tokens, feats = x_ref.shape
    width = feats * dp
    rows = tokens // CHUNKS
    head = q_s.shape[1]
    half = dp // 2
    scale = math.log2(math.e) / math.sqrt(head)

    barrier = pltpu.get_barrier_semaphore()
    for step in range(1, dp):
        pl.semaphore_signal(
            barrier, inc=1, device_id={"dp": lax.rem(p + step, dp)},
            device_id_type=pl.DeviceIdType.MESH,
        )
    for name, at in (("seq", 1 - y), ("section", 1 - sec)):
        pl.semaphore_signal(
            barrier, inc=1, device_id={name: at}, device_id_type=pl.DeviceIdType.MESH
        )

    def remote(src, dst, send, recv, where):
        return pltpu.make_async_remote_copy(
            src_ref=src, dst_ref=dst, send_sem=send, recv_sem=recv,
            device_id=where, device_id_type=pl.DeviceIdType.MESH,
        )

    def part(k):
        return pl.ds(k * rows, rows)

    def chunk(k):
        return pl.ds(pl.multiple_of(k * rows, rows), rows)

    own_x = pltpu.make_async_copy(x_ref, x_all.at[p], local.at[0])
    own_w = pltpu.make_async_copy(
        w_ref, w_all.at[pl.ds(pl.multiple_of(y * half * feats, feats), half * feats), :], local.at[1]
    )
    rand_copy = pltpu.make_async_copy(rand_ref, rand_s, local.at[2])
    rand_copy.start()
    own_x.start()
    own_w.start()
    g_all[p] = jnp.broadcast_to(gain_ref[...].astype(jnp.float32), (8, feats))

    pl.semaphore_wait(barrier, dp + 1)

    def hop(buf, send, recv, way, b, k, src=None):
        at = buf.at[b, part(k), :]
        to = (p - 2, p + 2, sib)[way]
        return remote(at if src is None else src, at, send.at[way, b, k], recv.at[b, k], {"dp": to})

    def spread(buf, send, recv, b, k, ways, act, src=None):
        if 0 in ways:
            @pl.when(z > 0)
            def _():
                act(hop(buf, send, recv, 0, b, k, src))
        if 1 in ways:
            @pl.when(z < nz - 1)
            def _():
                act(hop(buf, send, recv, 1, b, k, src))
        act(hop(buf, send, recv, 2, b, k, src))

    start = lambda copy: copy.start()
    sent = lambda copy: copy.wait_send()

    def chain(buf, send, recv, d, k):
        @pl.when(z + d < nz)
        def _():
            b = p + 2 * d
            hop(buf, send, recv, 2, b, k).wait_recv()
            spread(buf, send, recv, b, k, (0,), start)

        @pl.when(z - d >= 0)
        def _():
            b = p - 2 * d
            hop(buf, send, recv, 2, b, k).wait_recv()
            spread(buf, send, recv, b, k, (1,), start)

    def drain(buf, send, recv, k, src=None):
        spread(buf, send, recv, p, k, (0, 1), sent, src)
        for d in range(1, nz):
            @pl.when(z + d < nz)
            def _():
                spread(buf, send, recv, p + 2 * d, k, (0,), sent)

            @pl.when(z - d >= 0)
            def _():
                spread(buf, send, recv, p - 2 * d, k, (1,), sent)

    near = z // (nz // 2)
    far = 1 - near
    inward = 2 - 4 * near
    is_end = (z == 0) | (z == nz - 1)
    is_helper = jnp.logical_not(is_end)
    in_far, in_near = y == far, y != far
    mate, end, far_end = p + inward, p - inward, p + 2 * inward

    def other(b):
        return b + 1 - 2 * core

    def xhop(way, b, k, own=False):
        at = x_all.at[b, part(k), :]
        to = (p + inward, p - inward, sib)[way]
        src = x_ref.at[part(k), :] if own else at
        return remote(src, at, xs.at[way, b, k], xr.at[b, k], {"dp": to})

    def arrived(b, k, *ways):
        xhop(2, b, k).wait_recv()
        for way in ways:
            xhop(way, b, k).start()

    def rows_of(j):
        return pl.ds(pl.multiple_of(j * feats, feats), feats)

    def w_copy(j):
        return remote(
            w_ref.at[rows_of(j), :], w_all.at[rows_of(y * half + j), :], ws.at[j], wr.at[j],
            {"seq": 1 - y},
        )

    def far_copy(j, src, where):
        return remote(src, w_far.at[rows_of(j), :], fs.at[j], fr.at[j], where)

    def far_from_end(j):
        return far_copy(j, w_ref.at[rows_of(j), :], {"dp": mate})

    def far_passed(j):
        return far_copy(j, w_all.at[rows_of(far * half + j), :], {"dp": mate})

    def far_shared(j):
        return far_copy(j, w_far.at[rows_of(j), :], {"seq": 1 - y})

    def gain_copy(to, src):
        return remote(g_all.at[src], g_all.at[src], gs.at[to], gr.at[src], {"dp": to})

    quarter = half // 2
    first_w = (1 - y) * quarter
    rest_w = y * quarter

    @pl.when(is_helper)
    def _():
        for k in range(CHUNKS):
            for way in (0, 1, 2):
                xhop(way, p, k, True).start()
        for j in range(quarter):
            w_copy(first_w + j).start()

    @pl.when(is_end & in_far)
    def _():
        far_from_end(0).start()
        w_copy(quarter).start()
        for k in range(CHUNKS):
            xhop(2, p, k, True).start()

    @pl.when(is_end & in_near)
    def _():
        xhop(0, p, 0, True).start()
        for k in range(CHUNKS):
            xhop(2, p, k, True).start()
        for j in range(half):
            w_copy(j).start()

    for step in range(1, dp):
        gain_copy(lax.rem(p + step, dp), p).start()

    next_x = remote(x_ref, x_next, ns.at[0], nr.at[0], {"section": 1 - sec})
    next_w = remote(ow_ref, ow_next, ns.at[1], nr.at[1], {"section": 1 - sec})
    next_x.start()
    next_w.start()

    acc[...] = jnp.zeros_like(acc)

    rand_copy.wait()

    blocks = tokens // BLOCK
    for h in range(2):
        key_at = y if h == 0 else 1 - y
        lane = lax.broadcasted_iota(jnp.int32, (blocks, tokens), 1)
        key_id = lane // BLOCK + key_at * blocks
        query_id = lax.broadcasted_iota(jnp.int32, (blocks, tokens), 0) + y * blocks
        allowed = jnp.abs(query_id - key_id) <= 1
        for g in range(glob_ref.shape[1]):
            number = glob_ref[:, g : g + 1]
            allowed = allowed | (key_id == number) | (query_id == number)
        for r in range(rand_ref.shape[2]):
            allowed = allowed | (key_id == rand_s[0, :, r : r + 1])
        bias[h] = jnp.where(allowed, 0.0, -jnp.inf)

    def scaled(b, k):
        return (x_all[b, chunk(k), :].astype(jnp.float32) * g_all[b, 0:1, :]).astype(jnp.bfloat16)

    def project(b, k):
        acc[chunk(k), :] += jnp.dot(
            scaled(b, k), w_all[rows_of(b), :], preferred_element_type=jnp.float32
        )

    def project_whole(b):
        def body(i, _):
            at = pl.ds(pl.multiple_of(i * 2 * rows, 2 * rows), 2 * rows)
            xg = (x_all[b, at, :].astype(jnp.float32) * g_all[b, 0:1, :]).astype(jnp.bfloat16)
            acc[at, :] += jnp.dot(xg, w_all[rows_of(b), :], preferred_element_type=jnp.float32)
            return 0

        lax.fori_loop(0, CHUNKS // 2, body, 0)

    def from_sib(b, k):
        xhop(2, b, k).wait_recv()

    def kv_copy(k):
        return remote(kv.at[0, part(k), :], kv.at[1, part(k), :], ks.at[k], kr.at[k], {"seq": 1 - y})

    def finish_joined(k, joined, total):
        joined = joined * lax.rsqrt(total / width + 1e-05)
        q_s[part(k), :] = joined[:, :head].astype(jnp.bfloat16)
        kv[0, part(k), :] = joined[:, head:].astype(jnp.bfloat16)
        kv_copy(k).start()

    def part_copies(k):
        return (
            remote(part_out.at[part(k), :], part_in.at[part(k), :], ps.at[0, k], pr.at[0, k], {"dp": end}),
            remote(ss_out.at[k], ss_in.at[k], ps.at[1, k], pr.at[1, k], {"dp": end}),
        )

    def diagonal():
        return lax.broadcasted_iota(jnp.int32, (rows, rows), 0) == lax.broadcasted_iota(
            jnp.int32, (rows, rows), 1
        )

    def help_end(k):
        if k == 0:
            @pl.when(in_far)
            def _():
                for j in range(quarter, half):
                    far_shared(j).wait_recv()

            @pl.when(in_near)
            def _():
                for j in range(quarter):
                    far_shared(j).wait_recv()

        from_sib(other(end), k)
        from_sib(other(far_end), k)
        part_sum = jnp.zeros((rows, acc.shape[1]), jnp.float32)
        for j in range(half):
            part_sum += jnp.dot(
                scaled(far * half + j, k), w_far[pl.ds(j * feats, feats), :],
                preferred_element_type=jnp.float32,
            )
        part_out[part(k), :] = part_sum.astype(jnp.bfloat16)
        folded = jnp.zeros((rows, 128), jnp.float32)
        for b in range(dp):
            for c in range(feats // 128):
                xb = x_all[b, part(k), c * 128 : (c + 1) * 128].astype(jnp.float32)
                folded += xb * xb
        total = jnp.sum(folded, axis=1, keepdims=True)
        total_s[part(k), :] = total
        across = jnp.sum(
            jnp.where(diagonal(), jnp.broadcast_to(total, (rows, rows)), 0.0), axis=0, keepdims=True
        )
        ss_out[k] = jnp.broadcast_to(across, (8, rows))
        for copy in part_copies(k):
            copy.start()

    def all_gains():
        for step in range(1, dp):
            gain_copy(sib, lax.rem(p + step, dp)).wait_recv()

    @pl.when(is_end)
    def _():
        @pl.when(in_far)
        def _():
            for j in range(1, quarter):
                far_from_end(j - 1).wait_send()
                far_from_end(j).start()
                w_copy(quarter + j - 1).wait_send()
                w_copy(quarter + j).start()
            far_from_end(quarter - 1).wait_send()
            xhop(0, p, 0, True).start()

        @pl.when(in_near)
        def _():
            w_copy(quarter).wait_recv()
            xhop(0, p, 0, True).wait_send()
            far_passed(quarter).start()
            for j in range(quarter + 1, half):
                w_copy(j).wait_recv()
                far_passed(j - 1).wait_send()
                far_passed(j).start()

        for k in range(CHUNKS):
            arrived(mate, k, 2)

        @pl.when(in_far)
        def _():
            xhop(0, p, 0, True).wait_send()

        @pl.when(in_near)
        def _():
            far_passed(half - 1).wait_send()

        for k in range(1, CHUNKS):
            xhop(0, p, k, True).start()
            if k < CHUNKS - 1:
                xhop(0, p, k, True).wait_send()
        own_x.wait()
        own_w.wait()
        all_gains()

        @pl.when(in_far)
        def _():
            for j in range(half):
                w_copy(j).wait_recv()

        for k in range(CHUNKS):
            from_sib(sib, k)
            from_sib(other(mate), k)
        for b in (p, sib, mate, other(mate)):
            project_whole(b)
        for k in range(CHUNKS):
            for copy in part_copies(k):
                copy.wait_recv()
            total = jnp.sum(
                jnp.where(diagonal(), jnp.broadcast_to(ss_in[k, 0:1, :], (rows, rows)), 0.0),
                axis=1, keepdims=True,
            )
            finish_joined(k, acc[part(k), :] + part_in[part(k), :].astype(jnp.float32), total)

    @pl.when(is_helper)
    def _():
        def share(j):
            far_shared(j).wait_recv()
            far_shared(j).start()

        def when_far(fn):
            pl.when(in_far)(fn)

        def when_near(fn):
            pl.when(in_near)(fn)

        when_near(lambda: arrived(end, 0, 0, 2))
        when_far(lambda: share(0))
        when_far(lambda: share(1))
        when_near(lambda: share(2))
        for k in range(CHUNKS):
            arrived(mate, k, 2)
        when_far(lambda: arrived(end, 0, 0, 2))
        when_near(lambda: share(3))

        own_x.wait()
        own_w.wait()
        all_gains()
        for j in range(quarter):
            w_copy(rest_w + j).wait_recv()
        for k in range(CHUNKS):
            from_sib(sib, k)
            from_sib(other(mate), k)
        project_whole(p)
        project_whole(sib)
        arrived(end, 1, 0, 2)
        project_whole(mate)
        project_whole(other(mate))
        arrived(end, 2, 0, 2)

        @pl.when(in_far)
        def _():
            for j in range(quarter):
                far_shared(j).wait_send()

        @pl.when(in_near)
        def _():
            for j in range(quarter, half):
                far_shared(j).wait_send()

        for j in range(quarter):
            w_copy(rest_w + j).start()

        held = jnp.where(near == y, end, far_end)
        missing = jnp.where(near == y, far_end, end)

        def help_and_project(k):
            help_end(k)
            project(held, k)
            project(other(held), k)

        for k in range(CHUNKS):
            if k == 2:
                arrived(end, 3, 0, 2)
            arrived(far_end, k, 2)
            if k > 0:
                help_and_project(k - 1)
        help_and_project(CHUNKS - 1)
        for j in range(quarter):
            w_copy(first_w + j).wait_recv()
        for k in range(CHUNKS):
            project(missing, k)
            project(other(missing), k)
            finish_joined(k, acc[part(k), :], total_s[part(k), :])

    per = blocks // CHUNKS

    def scores_of(k, h, count):
        s = lax.dot_general(
            q_s[pl.ds(k * rows, count * rows), :], kv[h, :, :head], (((1,), (1,)), ((), ())),
            preferred_element_type=jnp.float32,
        )
        s = (s * scale).reshape(count * per, BLOCK, tokens)
        s = s + bias[h, k * per : (k + count) * per, :][:, None, :]
        return s.reshape(count * rows, tokens)

    def own_keys(k, count):
        at = pl.ds(k * rows, count * rows)
        s = scores_of(k, 0, count)
        m = jnp.max(s, axis=1, keepdims=True)
        e = jnp.exp2(s - m)
        m_s[at, :] = m
        l_s[at, :] = jnp.sum(e, axis=1, keepdims=True)
        o_s[at, :] = jnp.dot(
            e.astype(jnp.bfloat16), kv[0, :, head:], preferred_element_type=jnp.float32
        )

    def att_copy(k):
        return remote(
            att_own.at[part(k), :], att_all.at[p, part(k), :], ts.at[k], ar.at[p, k], {"section": 1 - sec}
        )

    def other_keys(k):
        s = scores_of(k, 1, 1)
        before = m_s[part(k), :]
        m = jnp.maximum(before, jnp.max(s, axis=1, keepdims=True))
        e = jnp.exp2(s - m)
        shrink = jnp.exp2(before - m)
        total = l_s[part(k), :] * shrink + jnp.sum(e, axis=1, keepdims=True)
        o = o_s[part(k), :] * shrink + jnp.dot(
            e.astype(jnp.bfloat16), kv[1, :, head:], preferred_element_type=jnp.float32
        )
        att_own[part(k), :] = (o / total).astype(jnp.bfloat16)
        att_copy(k).start()

    own_keys(0, CHUNKS // 2)
    for k in range(CHUNKS):
        kv_copy(k).wait_recv()

    def att_step(d, k):
        if d == 0:
            att_copy(k).wait_recv()
            spread(att_all, as_, ar, p, k, (0, 1), start)
        else:
            chain(att_all, as_, ar, d, k)

    def finish(k):
        hop(att_all, as_, ar, 2, sib, k).wait_recv()
        for d in range(1, nz):
            @pl.when(z + d < nz)
            def _():
                hop(att_all, as_, ar, 2, sib + 2 * d, k).wait_recv()

            @pl.when(z - d >= 0)
            def _():
                hop(att_all, as_, ar, 2, sib - 2 * d, k).wait_recv()
        heads = jnp.concatenate([att_all[b, part(k), :] for b in range(dp)], axis=1)
        added = jnp.dot(heads, ow_next[...], preferred_element_type=jnp.float32)
        out_ref[part(k), :] = (x_next[part(k), :].astype(jnp.float32) + added).astype(jnp.bfloat16)

    for i in range(CHUNKS + nz + 1):
        if i < CHUNKS:
            other_keys(i)
        if i == CHUNKS // 2 - 1:
            own_keys(CHUNKS // 2, CHUNKS // 2)
        for d in range(nz):
            if 0 <= i - 1 - d < CHUNKS:
                att_step(d, i - 1 - d)
        if i == nz + 1:
            next_x.wait_recv()
            next_w.wait_recv()
        if 0 <= i - nz - 1 < CHUNKS:
            finish(i - nz - 1)

    for k in range(CHUNKS):
        drain(att_all, as_, ar, k)
        kv_copy(k).wait_send()
        att_copy(k).wait_send()
        xhop(2, p, k, True).wait_send()
        xhop(2, mate, k).wait_send()

        @pl.when(is_helper)
        def _():
            xhop(0, p, k, True).wait_send()
            xhop(1, p, k, True).wait_send()
            xhop(0, end, k).wait_send()
            xhop(2, end, k).wait_send()
            xhop(2, far_end, k).wait_send()
            for copy in part_copies(k):
                copy.wait_send()

    for step in range(1, dp):
        gain_copy(lax.rem(p + step, dp), p).wait_send()
    @pl.when(is_end)
    def _():
        xhop(0, p, CHUNKS - 1, True).wait_send()

    @pl.when(is_end & in_far)
    def _():
        w_copy(half - 1).wait_send()

    @pl.when(jnp.logical_not(is_end & in_far))
    def _():
        for j in range(half):
            w_copy(j).wait_send()

    next_x.wait_send()
    next_w.wait_send()


def relay(dp, x, gain, w, ow, rand, glob):
    nz = dp // 2
    tokens, feats = x.shape
    columns = w.shape[1]
    head = columns // 3
    vmem = pl.BlockSpec(memory_space=pltpu.VMEM)
    anywhere = pl.BlockSpec(memory_space=pl.ANY)
    bf16, f32, dma = jnp.bfloat16, jnp.float32, pltpu.SemaphoreType.DMA
    return pl.pallas_call(
        functools.partial(relay_kernel, nz),
        out_shape=jax.ShapeDtypeStruct((tokens, feats), bf16),
        in_specs=[anywhere, vmem, anywhere, anywhere, anywhere, vmem],
        out_specs=vmem,
        scratch_shapes=[
            pltpu.VMEM((dp, tokens, feats), bf16),
            pltpu.VMEM((dp * feats, columns), bf16),
            pltpu.VMEM((dp, 8, feats), f32),
            pltpu.VMEM((tokens, columns), f32),
            pltpu.VMEM((tokens, head), bf16),
            pltpu.VMEM((2, tokens, 2 * head), bf16),
            pltpu.VMEM((2, tokens // BLOCK, tokens), f32),
            pltpu.VMEM((tokens, 1), f32),
            pltpu.VMEM((tokens, 1), f32),
            pltpu.VMEM((tokens, head), f32),
            pltpu.VMEM((tokens, head), bf16),
            pltpu.VMEM((dp, tokens, head), bf16),
            pltpu.VMEM((tokens, feats), bf16),
            pltpu.VMEM(ow.shape, bf16),
            pltpu.VMEM((dp // 2 * feats, columns), bf16),
            pltpu.VMEM((tokens, columns), bf16),
            pltpu.VMEM((tokens, columns), bf16),
            pltpu.VMEM((CHUNKS, 8, tokens // CHUNKS), f32),
            pltpu.VMEM((CHUNKS, 8, tokens // CHUNKS), f32),
            pltpu.VMEM((tokens, 1), f32),
            pltpu.VMEM(rand.shape, jnp.int32),
            dma((3, dp, CHUNKS)),
            dma((dp, CHUNKS)),
            dma((dp // 2,)),
            dma((dp // 2,)),
            dma((dp,)),
            dma((dp,)),
            dma((CHUNKS,)),
            dma((CHUNKS,)),
            dma((CHUNKS,)),
            dma((CHUNKS,)),
            dma((3, dp, CHUNKS)),
            dma((dp, CHUNKS)),
            dma((2,)),
            dma((2,)),
            dma((dp // 2,)),
            dma((dp // 2,)),
            dma((2, CHUNKS)),
            dma((2, CHUNKS)),
            dma((3,)),
        ],
        compiler_params=pltpu.CompilerParams(
            collective_id=0, has_side_effects=True, vmem_limit_bytes=56 * 1024 * 1024
        ),
        name="relay_layer",
    )(x, gain, w, ow, rand, glob)


def tiles(mesh, tokens, feats, columns):
    return (
        mesh.shape["section"] == 2
        and mesh.shape["seq"] == 2
        and mesh.shape["dp"] == 8
        and feats % 128 == 0
        and columns % 384 == 0
        and tokens % (CHUNKS * BLOCK) == 0
    )


def solution(mesh):
    placed = (
        P("section", "seq", "dp"),
        P("section", "dp"),
        P("section", "seq", "dp"),
        P("section", None, "dp"),
        P("section", "seq", None),
        P("section", None),
    )

    def layer(section_input, norm_gain, qkv_weight, out_weight, random_blocks, global_blocks):
        args = (section_input, norm_gain, qkv_weight, out_weight, random_blocks, global_blocks)
        _, tokens, feats = section_input.shape
        if not tiles(mesh, tokens, feats, qkv_weight.shape[2]):
            return shards(*args)
        out = relay(
            mesh.shape["dp"], section_input[0], norm_gain, qkv_weight[0], out_weight[0],
            random_blocks, global_blocks,
        )
        return out[None]

    return jax.shard_map(
        layer, mesh=mesh, in_specs=placed, out_specs=P("section", "seq", "dp"), check_vma=False
    )
```

```python
import functools
import math

import jax
import jax.numpy as jnp
from jax import lax
from jax.experimental import pallas as pl
from jax.experimental.pallas import tpu as pltpu
from jax.sharding import PartitionSpec as P

BLOCK = 64


def shifted(block, axis, distance):
    devices = range(lax.axis_size(axis))
    route = [((i - distance) % len(devices), i) for i in devices]
    return lax.ppermute(block, axis, route)


def block_mask(query_ids, random_rows, global_ids, key_count):
    query_col = query_ids[:, None]
    key_ids = jnp.arange(key_count, dtype=jnp.int32)[None, :]
    adjacent = jnp.abs(query_col - key_ids) <= 1
    key_global = jnp.any(key_ids[:, :, None] == global_ids[None, None, :], axis=2)
    query_global = jnp.any(query_col[:, :, None] == global_ids[None, None, :], axis=2)
    chosen = jnp.any(random_rows[:, None, :] == key_ids[:, :, None], axis=2)
    return adjacent | key_global | query_global | chosen


def sparse_attention(query, keys, values, allowed, block_size):
    scores = lax.dot_general(
        query, keys, (((1,), (1,)), ((), ())), preferred_element_type=jnp.float32
    )
    scores = scores * (1.0 / math.sqrt(query.shape[1]))
    query_blocks, key_blocks = allowed.shape
    scores = scores.reshape(query_blocks, block_size, key_blocks, block_size)
    live = allowed[:, None, :, None]
    scores = jnp.where(live, scores, -1e30)
    highest = jnp.max(scores, axis=(2, 3), keepdims=True)
    weights = jnp.where(live, jnp.exp(scores - highest), 0.0)
    totals = jnp.sum(weights, axis=(2, 3), keepdims=True)
    probs = (
        (weights / totals)
        .reshape(query_blocks * block_size, key_blocks * block_size)
        .astype(jnp.bfloat16)
    )
    return jnp.dot(probs, values, preferred_element_type=jnp.float32).astype(jnp.bfloat16)


def shards(section_input, norm_gain, qkv_weight, out_weight, random_blocks, global_blocks):
    token_rows = section_input[0]
    token_count = token_rows.shape[0]
    width = norm_gain.shape[1] * lax.axis_size("dp")
    as_float = token_rows.astype(jnp.float32)
    local_squares = jnp.sum(as_float * as_float, axis=1)
    total_squares = lax.psum(local_squares, "dp")
    factor = lax.rsqrt(total_squares / width + 1e-05)[:, None]
    normed_part = (as_float * factor * norm_gain[0].astype(jnp.float32)).astype(jnp.bfloat16)
    normed = lax.all_gather(normed_part, "dp", axis=1, tiled=True)
    weight_half = qkv_weight[0]
    joined = jnp.dot(
        normed,
        lax.all_gather(weight_half, "seq", axis=0, tiled=True),
        preferred_element_type=jnp.float32,
    )
    head_size = joined.shape[1] // 3
    query = joined[:, :head_size].astype(jnp.bfloat16)
    keys_values = joined[:, head_size:].astype(jnp.bfloat16)
    document_kv = lax.all_gather(keys_values, "seq", axis=0, tiled=True)
    keys = document_kv[:, :head_size]
    values = document_kv[:, head_size:]
    own_blocks = token_count // BLOCK
    query_ids = lax.axis_index("seq") * own_blocks + jnp.arange(own_blocks, dtype=jnp.int32)
    allowed = block_mask(
        query_ids, random_blocks[0], global_blocks[0], document_kv.shape[0] // BLOCK
    )
    attended = sparse_attention(query, keys, values, allowed, BLOCK)
    out_columns = out_weight[0]
    added = jnp.dot(
        lax.all_gather(attended, "dp", axis=1, tiled=True),
        out_columns,
        preferred_element_type=jnp.float32,
    )
    result = (token_rows.astype(jnp.float32) + added).astype(jnp.bfloat16)
    return shifted(result[None], "section", 1)


CHUNKS = 4


def relay_kernel(
    nz,
    x_ref,
    gain_ref,
    w_ref,
    ow_ref,
    rand_ref,
    glob_ref,
    out_ref,
    x_all,
    w_all,
    g_all,
    acc,
    q_s,
    kv,
    bias,
    m_s,
    l_s,
    o_s,
    att_own,
    att_all,
    x_next,
    ow_next,
    w_far,
    part_out,
    part_in,
    ss_out,
    ss_in,
    total_s,
    rand_s,
    xs,
    xr,
    ws,
    wr,
    gs,
    gr,
    ks,
    kr,
    ts,
    tr,
    as_,
    ar,
    ns,
    nr,
    fs,
    fr,
    ps,
    pr,
    local,
):
    sec, p, y = lax.axis_index("section"), lax.axis_index("dp"), lax.axis_index("seq")
    dp = 2 * nz
    z, core = p // 2, p % 2
    sib = p + 1 - 2 * core
    tokens, feats = x_ref.shape
    width = feats * dp
    rows = tokens // CHUNKS
    head = q_s.shape[1]
    half = dp // 2
    scale = math.log2(math.e) / math.sqrt(head)

    barrier = pltpu.get_barrier_semaphore()
    for step in range(1, dp):
        pl.semaphore_signal(
            barrier, inc=1, device_id={"dp": lax.rem(p + step, dp)},
            device_id_type=pl.DeviceIdType.MESH,
        )
    for name, at in (("seq", 1 - y), ("section", 1 - sec)):
        pl.semaphore_signal(
            barrier, inc=1, device_id={name: at}, device_id_type=pl.DeviceIdType.MESH
        )

    def remote(src, dst, send, recv, where):
        return pltpu.make_async_remote_copy(
            src_ref=src, dst_ref=dst, send_sem=send, recv_sem=recv,
            device_id=where, device_id_type=pl.DeviceIdType.MESH,
        )

    def part(k):
        return pl.ds(k * rows, rows)

    def chunk(k):
        return pl.ds(pl.multiple_of(k * rows, rows), rows)

    own_x = pltpu.make_async_copy(x_ref, x_all.at[p], local.at[0])
    own_w = pltpu.make_async_copy(
        w_ref, w_all.at[pl.ds(pl.multiple_of(y * half * feats, feats), half * feats), :], local.at[1]
    )
    rand_copy = pltpu.make_async_copy(rand_ref, rand_s, local.at[2])
    rand_copy.start()
    own_x.start()
    own_w.start()
    g_all[p] = jnp.broadcast_to(gain_ref[...].astype(jnp.float32), (8, feats))

    pl.semaphore_wait(barrier, dp + 1)

    def hop(buf, send, recv, way, b, k, src=None):
        at = buf.at[b, part(k), :]
        to = (p - 2, p + 2, sib)[way]
        return remote(at if src is None else src, at, send.at[way, b, k], recv.at[b, k], {"dp": to})

    def spread(buf, send, recv, b, k, ways, act, src=None):
        if 0 in ways:
            @pl.when(z > 0)
            def _():
                act(hop(buf, send, recv, 0, b, k, src))
        if 1 in ways:
            @pl.when(z < nz - 1)
            def _():
                act(hop(buf, send, recv, 1, b, k, src))
        act(hop(buf, send, recv, 2, b, k, src))

    start = lambda copy: copy.start()
    sent = lambda copy: copy.wait_send()

    def chain(buf, send, recv, d, k):
        @pl.when(z + d < nz)
        def _():
            b = p + 2 * d
            hop(buf, send, recv, 2, b, k).wait_recv()
            spread(buf, send, recv, b, k, (0,), start)

        @pl.when(z - d >= 0)
        def _():
            b = p - 2 * d
            hop(buf, send, recv, 2, b, k).wait_recv()
            spread(buf, send, recv, b, k, (1,), start)

    def drain(buf, send, recv, k, src=None):
        spread(buf, send, recv, p, k, (0, 1), sent, src)
        for d in range(1, nz):
            @pl.when(z + d < nz)
            def _():
                spread(buf, send, recv, p + 2 * d, k, (0,), sent)

            @pl.when(z - d >= 0)
            def _():
                spread(buf, send, recv, p - 2 * d, k, (1,), sent)

    near = z // (nz // 2)
    far = 1 - near
    inward = 2 - 4 * near
    is_end = (z == 0) | (z == nz - 1)
    is_helper = jnp.logical_not(is_end)
    in_far, in_near = y == far, y != far
    mate, end, far_end = p + inward, p - inward, p + 2 * inward

    def other(b):
        return b + 1 - 2 * core

    def xhop(way, b, k, own=False):
        at = x_all.at[b, part(k), :]
        to = (p + inward, p - inward, sib)[way]
        src = x_ref.at[part(k), :] if own else at
        return remote(src, at, xs.at[way, b, k], xr.at[b, k], {"dp": to})

    def arrived(b, k, *ways):
        xhop(2, b, k).wait_recv()
        for way in ways:
            xhop(way, b, k).start()

    def rows_of(j):
        return pl.ds(pl.multiple_of(j * feats, feats), feats)

    def w_copy(j):
        return remote(
            w_ref.at[rows_of(j), :], w_all.at[rows_of(y * half + j), :], ws.at[j], wr.at[j],
            {"seq": 1 - y},
        )

    def far_copy(j, src, where):
        return remote(src, w_far.at[rows_of(j), :], fs.at[j], fr.at[j], where)

    def far_from_end(j):
        return far_copy(j, w_ref.at[rows_of(j), :], {"dp": mate})

    def far_passed(j):
        return far_copy(j, w_all.at[rows_of(far * half + j), :], {"dp": mate})

    def far_shared(j):
        return far_copy(j, w_far.at[rows_of(j), :], {"seq": 1 - y})

    def gain_copy(to, src):
        return remote(g_all.at[src], g_all.at[src], gs.at[to], gr.at[src], {"dp": to})

    quarter = half // 2
    first_w = (1 - y) * quarter
    rest_w = y * quarter

    @pl.when(is_helper)
    def _():
        for k in range(CHUNKS):
            for way in (0, 1, 2):
                xhop(way, p, k, True).start()
        for j in range(quarter):
            w_copy(first_w + j).start()

    @pl.when(is_end & in_far)
    def _():
        far_from_end(0).start()
        w_copy(quarter).start()
        for k in range(CHUNKS):
            xhop(2, p, k, True).start()

    @pl.when(is_end & in_near)
    def _():
        xhop(0, p, 0, True).start()
        for k in range(CHUNKS):
            xhop(2, p, k, True).start()
        for j in range(half):
            w_copy(j).start()

    for step in range(1, dp):
        gain_copy(lax.rem(p + step, dp), p).start()

    next_x = remote(x_ref, x_next, ns.at[0], nr.at[0], {"section": 1 - sec})
    next_w = remote(ow_ref, ow_next, ns.at[1], nr.at[1], {"section": 1 - sec})
    next_x.start()
    next_w.start()

    acc[...] = jnp.zeros_like(acc)

    rand_copy.wait()

    blocks = tokens // BLOCK
    for h in range(2):
        key_at = y if h == 0 else 1 - y
        lane = lax.broadcasted_iota(jnp.int32, (blocks, tokens), 1)
        key_id = lane // BLOCK + key_at * blocks
        query_id = lax.broadcasted_iota(jnp.int32, (blocks, tokens), 0) + y * blocks
        allowed = jnp.abs(query_id - key_id) <= 1
        for g in range(glob_ref.shape[1]):
            number = glob_ref[:, g : g + 1]
            allowed = allowed | (key_id == number) | (query_id == number)
        for r in range(rand_ref.shape[2]):
            allowed = allowed | (key_id == rand_s[0, :, r : r + 1])
        bias[h] = jnp.where(allowed, 0.0, -jnp.inf)

    def scaled(b, k):
        return (x_all[b, chunk(k), :].astype(jnp.float32) * g_all[b, 0:1, :]).astype(jnp.bfloat16)

    def project(b, k):
        acc[chunk(k), :] += jnp.dot(
            scaled(b, k), w_all[rows_of(b), :], preferred_element_type=jnp.float32
        )

    def project_whole(b):
        def body(i, _):
            at = pl.ds(pl.multiple_of(i * 2 * rows, 2 * rows), 2 * rows)
            xg = (x_all[b, at, :].astype(jnp.float32) * g_all[b, 0:1, :]).astype(jnp.bfloat16)
            acc[at, :] += jnp.dot(xg, w_all[rows_of(b), :], preferred_element_type=jnp.float32)
            return 0

        lax.fori_loop(0, CHUNKS // 2, body, 0)

    def from_sib(b, k):
        xhop(2, b, k).wait_recv()

    def kv_copy(k):
        return remote(kv.at[0, part(k), :], kv.at[1, part(k), :], ks.at[k], kr.at[k], {"seq": 1 - y})

    def finish_joined(k, joined, total):
        joined = joined * lax.rsqrt(total / width + 1e-05)
        q_s[part(k), :] = joined[:, :head].astype(jnp.bfloat16)
        kv[0, part(k), :] = joined[:, head:].astype(jnp.bfloat16)
        kv_copy(k).start()

    def part_copies(k):
        return (
            remote(part_out.at[part(k), :], part_in.at[part(k), :], ps.at[0, k], pr.at[0, k], {"dp": end}),
            remote(ss_out.at[k], ss_in.at[k], ps.at[1, k], pr.at[1, k], {"dp": end}),
        )

    def diagonal():
        return lax.broadcasted_iota(jnp.int32, (rows, rows), 0) == lax.broadcasted_iota(
            jnp.int32, (rows, rows), 1
        )

    def help_end(k):
        if k == 0:
            @pl.when(in_far)
            def _():
                for j in range(quarter, half):
                    far_shared(j).wait_recv()

            @pl.when(in_near)
            def _():
                for j in range(quarter):
                    far_shared(j).wait_recv()

        from_sib(other(end), k)
        from_sib(other(far_end), k)
        part_sum = jnp.zeros((rows, acc.shape[1]), jnp.float32)
        for j in range(half):
            part_sum += jnp.dot(
                scaled(far * half + j, k), w_far[pl.ds(j * feats, feats), :],
                preferred_element_type=jnp.float32,
            )
        part_out[part(k), :] = part_sum.astype(jnp.bfloat16)
        folded = jnp.zeros((rows, 128), jnp.float32)
        for b in range(dp):
            for c in range(feats // 128):
                xb = x_all[b, part(k), c * 128 : (c + 1) * 128].astype(jnp.float32)
                folded += xb * xb
        total = jnp.sum(folded, axis=1, keepdims=True)
        total_s[part(k), :] = total
        across = jnp.sum(
            jnp.where(diagonal(), jnp.broadcast_to(total, (rows, rows)), 0.0), axis=0, keepdims=True
        )
        ss_out[k] = jnp.broadcast_to(across, (8, rows))
        for copy in part_copies(k):
            copy.start()

    def all_gains():
        for step in range(1, dp):
            gain_copy(sib, lax.rem(p + step, dp)).wait_recv()

    @pl.when(is_end)
    def _():
        @pl.when(in_far)
        def _():
            for j in range(1, quarter):
                far_from_end(j - 1).wait_send()
                far_from_end(j).start()
                w_copy(quarter + j - 1).wait_send()
                w_copy(quarter + j).start()
            far_from_end(quarter - 1).wait_send()
            xhop(0, p, 0, True).start()

        @pl.when(in_near)
        def _():
            w_copy(quarter).wait_recv()
            xhop(0, p, 0, True).wait_send()
            far_passed(quarter).start()
            for j in range(quarter + 1, half):
                w_copy(j).wait_recv()
                far_passed(j - 1).wait_send()
                far_passed(j).start()

        for k in range(CHUNKS):
            arrived(mate, k, 2)

        @pl.when(in_far)
        def _():
            xhop(0, p, 0, True).wait_send()

        @pl.when(in_near)
        def _():
            far_passed(half - 1).wait_send()

        for k in range(1, CHUNKS):
            xhop(0, p, k, True).start()
            if k < CHUNKS - 1:
                xhop(0, p, k, True).wait_send()
        own_x.wait()
        own_w.wait()
        all_gains()

        @pl.when(in_far)
        def _():
            for j in range(half):
                w_copy(j).wait_recv()

        for k in range(CHUNKS):
            from_sib(sib, k)
            from_sib(other(mate), k)
        for b in (p, sib, mate, other(mate)):
            project_whole(b)
        for k in range(CHUNKS):
            for copy in part_copies(k):
                copy.wait_recv()
            total = jnp.sum(
                jnp.where(diagonal(), jnp.broadcast_to(ss_in[k, 0:1, :], (rows, rows)), 0.0),
                axis=1, keepdims=True,
            )
            finish_joined(k, acc[part(k), :] + part_in[part(k), :].astype(jnp.float32), total)

    @pl.when(is_helper)
    def _():
        def share(j):
            far_shared(j).wait_recv()
            far_shared(j).start()

        def when_far(fn):
            pl.when(in_far)(fn)

        def when_near(fn):
            pl.when(in_near)(fn)

        when_near(lambda: arrived(end, 0, 0, 2))
        when_far(lambda: share(0))
        when_far(lambda: share(1))
        when_near(lambda: share(2))
        for k in range(CHUNKS):
            arrived(mate, k, 2)
        when_far(lambda: arrived(end, 0, 0, 2))
        when_near(lambda: share(3))

        own_x.wait()
        own_w.wait()
        all_gains()
        for j in range(quarter):
            w_copy(rest_w + j).wait_recv()
        for k in range(CHUNKS):
            from_sib(sib, k)
            from_sib(other(mate), k)
        project_whole(p)
        project_whole(sib)
        arrived(end, 1, 0, 2)
        project_whole(mate)
        project_whole(other(mate))

        @pl.when(in_far)
        def _():
            for j in range(quarter):
                far_shared(j).wait_send()

        @pl.when(in_near)
        def _():
            for j in range(quarter, half):
                far_shared(j).wait_send()

        for j in range(quarter):
            w_copy(rest_w + j).start()
        arrived(end, 2, 0, 2)

        held = jnp.where(near == y, end, far_end)
        missing = jnp.where(near == y, far_end, end)

        def help_and_project(k):
            help_end(k)
            project(held, k)
            project(other(held), k)

        for k in range(CHUNKS):
            if k == 2:
                arrived(end, 3, 0, 2)
            arrived(far_end, k, 2)
            if k > 0:
                help_and_project(k - 1)
        help_and_project(CHUNKS - 1)
        for j in range(quarter):
            w_copy(first_w + j).wait_recv()
        for k in range(CHUNKS):
            project(missing, k)
            project(other(missing), k)
            finish_joined(k, acc[part(k), :], total_s[part(k), :])

    per = blocks // CHUNKS

    def scores_of(k, h):
        s = lax.dot_general(
            q_s[part(k), :], kv[h, :, :head], (((1,), (1,)), ((), ())),
            preferred_element_type=jnp.float32,
        )
        s = (s * scale).reshape(per, BLOCK, tokens)
        s = s + bias[h, k * per : (k + 1) * per, :][:, None, :]
        return s.reshape(rows, tokens)

    def own_keys(k):
        s = scores_of(k, 0)
        m = jnp.max(s, axis=1, keepdims=True)
        e = jnp.exp2(s - m)
        m_s[part(k), :] = m
        l_s[part(k), :] = jnp.sum(e, axis=1, keepdims=True)
        o_s[part(k), :] = jnp.dot(
            e.astype(jnp.bfloat16), kv[0, :, head:], preferred_element_type=jnp.float32
        )

    def att_copy(k):
        return remote(
            att_own.at[part(k), :], att_all.at[p, part(k), :], ts.at[k], ar.at[p, k], {"section": 1 - sec}
        )

    def other_keys(k):
        s = scores_of(k, 1)
        before = m_s[part(k), :]
        m = jnp.maximum(before, jnp.max(s, axis=1, keepdims=True))
        e = jnp.exp2(s - m)
        shrink = jnp.exp2(before - m)
        total = l_s[part(k), :] * shrink + jnp.sum(e, axis=1, keepdims=True)
        o = o_s[part(k), :] * shrink + jnp.dot(
            e.astype(jnp.bfloat16), kv[1, :, head:], preferred_element_type=jnp.float32
        )
        att_own[part(k), :] = (o / total).astype(jnp.bfloat16)
        att_copy(k).start()

    for k in range(CHUNKS):
        own_keys(k)
    for k in range(CHUNKS):
        kv_copy(k).wait_recv()
    next_x.wait_recv()
    next_w.wait_recv()

    def att_step(d, k):
        if d == 0:
            att_copy(k).wait_recv()
            spread(att_all, as_, ar, p, k, (0, 1), start)
        else:
            chain(att_all, as_, ar, d, k)

    def finish(k):
        hop(att_all, as_, ar, 2, sib, k).wait_recv()
        for d in range(1, nz):
            @pl.when(z + d < nz)
            def _():
                hop(att_all, as_, ar, 2, sib + 2 * d, k).wait_recv()

            @pl.when(z - d >= 0)
            def _():
                hop(att_all, as_, ar, 2, sib - 2 * d, k).wait_recv()
        heads = jnp.concatenate([att_all[b, part(k), :] for b in range(dp)], axis=1)
        added = jnp.dot(heads, ow_next[...], preferred_element_type=jnp.float32)
        out_ref[part(k), :] = (x_next[part(k), :].astype(jnp.float32) + added).astype(jnp.bfloat16)

    for i in range(CHUNKS + nz + 1):
        if i < CHUNKS:
            other_keys(i)
        for d in range(nz):
            if 0 <= i - 1 - d < CHUNKS:
                att_step(d, i - 1 - d)
        if 0 <= i - nz - 1 < CHUNKS:
            finish(i - nz - 1)

    for k in range(CHUNKS):
        drain(att_all, as_, ar, k)
        kv_copy(k).wait_send()
        att_copy(k).wait_send()
        xhop(2, p, k, True).wait_send()
        xhop(2, mate, k).wait_send()

        @pl.when(is_helper)
        def _():
            xhop(0, p, k, True).wait_send()
            xhop(1, p, k, True).wait_send()
            xhop(0, end, k).wait_send()
            xhop(2, end, k).wait_send()
            xhop(2, far_end, k).wait_send()
            for copy in part_copies(k):
                copy.wait_send()

    for step in range(1, dp):
        gain_copy(lax.rem(p + step, dp), p).wait_send()
    @pl.when(is_end)
    def _():
        xhop(0, p, CHUNKS - 1, True).wait_send()

    @pl.when(is_end & in_far)
    def _():
        w_copy(half - 1).wait_send()

    @pl.when(jnp.logical_not(is_end & in_far))
    def _():
        for j in range(half):
            w_copy(j).wait_send()

    next_x.wait_send()
    next_w.wait_send()


def relay(dp, x, gain, w, ow, rand, glob):
    nz = dp // 2
    tokens, feats = x.shape
    columns = w.shape[1]
    head = columns // 3
    vmem = pl.BlockSpec(memory_space=pltpu.VMEM)
    anywhere = pl.BlockSpec(memory_space=pl.ANY)
    bf16, f32, dma = jnp.bfloat16, jnp.float32, pltpu.SemaphoreType.DMA
    return pl.pallas_call(
        functools.partial(relay_kernel, nz),
        out_shape=jax.ShapeDtypeStruct((tokens, feats), bf16),
        in_specs=[anywhere, vmem, anywhere, anywhere, anywhere, vmem],
        out_specs=vmem,
        scratch_shapes=[
            pltpu.VMEM((dp, tokens, feats), bf16),
            pltpu.VMEM((dp * feats, columns), bf16),
            pltpu.VMEM((dp, 8, feats), f32),
            pltpu.VMEM((tokens, columns), f32),
            pltpu.VMEM((tokens, head), bf16),
            pltpu.VMEM((2, tokens, 2 * head), bf16),
            pltpu.VMEM((2, tokens // BLOCK, tokens), f32),
            pltpu.VMEM((tokens, 1), f32),
            pltpu.VMEM((tokens, 1), f32),
            pltpu.VMEM((tokens, head), f32),
            pltpu.VMEM((tokens, head), bf16),
            pltpu.VMEM((dp, tokens, head), bf16),
            pltpu.VMEM((tokens, feats), bf16),
            pltpu.VMEM(ow.shape, bf16),
            pltpu.VMEM((dp // 2 * feats, columns), bf16),
            pltpu.VMEM((tokens, columns), bf16),
            pltpu.VMEM((tokens, columns), bf16),
            pltpu.VMEM((CHUNKS, 8, tokens // CHUNKS), f32),
            pltpu.VMEM((CHUNKS, 8, tokens // CHUNKS), f32),
            pltpu.VMEM((tokens, 1), f32),
            pltpu.VMEM(rand.shape, jnp.int32),
            dma((3, dp, CHUNKS)),
            dma((dp, CHUNKS)),
            dma((dp // 2,)),
            dma((dp // 2,)),
            dma((dp,)),
            dma((dp,)),
            dma((CHUNKS,)),
            dma((CHUNKS,)),
            dma((CHUNKS,)),
            dma((CHUNKS,)),
            dma((3, dp, CHUNKS)),
            dma((dp, CHUNKS)),
            dma((2,)),
            dma((2,)),
            dma((dp // 2,)),
            dma((dp // 2,)),
            dma((2, CHUNKS)),
            dma((2, CHUNKS)),
            dma((3,)),
        ],
        compiler_params=pltpu.CompilerParams(
            collective_id=0, has_side_effects=True, vmem_limit_bytes=56 * 1024 * 1024
        ),
        name="relay_layer",
    )(x, gain, w, ow, rand, glob)


def tiles(mesh, tokens, feats, columns):
    return (
        mesh.shape["section"] == 2
        and mesh.shape["seq"] == 2
        and mesh.shape["dp"] == 8
        and feats % 128 == 0
        and columns % 384 == 0
        and tokens % (CHUNKS * BLOCK) == 0
    )


def solution(mesh):
    placed = (
        P("section", "seq", "dp"),
        P("section", "dp"),
        P("section", "seq", "dp"),
        P("section", None, "dp"),
        P("section", "seq", None),
        P("section", None),
    )

    def layer(section_input, norm_gain, qkv_weight, out_weight, random_blocks, global_blocks):
        args = (section_input, norm_gain, qkv_weight, out_weight, random_blocks, global_blocks)
        _, tokens, feats = section_input.shape
        if not tiles(mesh, tokens, feats, qkv_weight.shape[2]):
            return shards(*args)
        out = relay(
            mesh.shape["dp"], section_input[0], norm_gain, qkv_weight[0], out_weight[0],
            random_blocks, global_blocks,
        )
        return out[None]

    return jax.shard_map(
        layer, mesh=mesh, in_specs=placed, out_specs=P("section", "seq", "dp"), check_vma=False
    )
```
